256 devices in a mesh: grp: 32 (over z_lo, x, core), tp: 8 (over y, z_hi).
Axes of the slice: x: 4, y: 4, z: 8 (z_hi: 2, z_lo: 4; z = z_hi * 4 + z_lo), core: 2. Of those that a mesh axis runs over, the one named last changes fastest.
Arguments:
- q_attn: bfloat16 [64, 64, 4096], P('grp', None, 'tp'), may hold values from -6 to 6
- q_resid: bfloat16 [64, 64, 4096], P('grp', None, 'tp'), may hold values from -6 to 6
- p_attn: bfloat16 [64, 128, 4096], P('grp', None, 'tp'), may hold values from -6 to 6
- p_resid: bfloat16 [64, 128, 4096], P('grp', None, 'tp'), may hold values from -6 to 6
- w_out: bfloat16 [4096, 4096], P('grp', 'tp'), may hold values from -0.09375 to 0.09375
- w_snap: bfloat16 [4096, 4096], P('grp', 'tp'), may hold values from -0.09375 to 0.09375
- norm_gain: bfloat16 [4096], P('tp'), may hold values from 0.25 to 4
- pass_attn: bfloat16 [64, 256, 4096], P('grp', None, 'tp'), may hold values from -6 to 6
- pass_resid: bfloat16 [64, 256, 4096], P('grp', None, 'tp'), may hold values from -6 to 6
- pass_len: int32 [64], P('grp'), may hold values from 128 to 256, as said below
- block_owner: int32 [32], replicated, may hold values from 0 to 31, each once
- neg_ids: int32 [64, 8], P('grp'), may hold values from 0 to 63
Outputs:
- loss: float32 [], replicated
- w_grad: float32 [4096, 4096], P('grp', 'tp')
- passage_index: bfloat16 [64, 4096], P('grp', 'tp')
The draws below stay inside these ranges and needn't reach their ends.
Inputs may be any that keep to these rules, and one draw needn't show every extreme that they name: `pass_len`: lengths are multiples of 128; in every block of 2 slots one passage has 256 tokens.
All inputs are finite; a program needn't handle non-finite values.
Results may differ from the reference program's by a relative error of at most 0.0034.
Values may be sent and summed in bfloat16 or wider, within the bound.
A program may use at most 64 MiB of HBM per device.

```python
import math
import jax
import jax.numpy as jnp
from jax import lax

D = 4096
QLEN = 64
POSLEN = 128
BLK = 2
BUCKET = 128
PLEN = 256
NNEG = 8
QUERIES = 64
PASSAGES = 64
BLOCKS = 32


def draw_pass_len(key, part):
    key = jax.random.fold_in(key, 11)
    first, second = jax.random.split(key)
    counts = jax.random.randint(first, (PASSAGES // BLK, BLK), 1, PLEN // BUCKET + 1)
    longest = jax.random.randint(second, (PASSAGES // BLK, 1), 0, BLK)
    counts = jnp.where(jnp.arange(BLK)[None, :] == longest, PLEN // BUCKET, counts)
    return (counts * BUCKET).reshape(PASSAGES).astype(jnp.int32)


def touch_ends(entries, stream_key, smallest, top_value):
    spot = [jax.random.randint(jax.random.fold_in(stream_key, axis), (), 0, length) for axis, length in enumerate(entries.shape)]
    main_axis = entries.shape.index(max(entries.shape))
    beside = spot[:main_axis] + [(spot[main_axis] + 1) % entries.shape[main_axis]] + spot[main_axis + 1:]
    return entries.at[tuple(spot)].set(smallest).at[tuple(beside)].set(top_value)


def steps_of(stream_key, shape, cuts, smallest, high):
    factor_of, own = 1.0, jax.random.fold_in(stream_key, 6)
    for dim, blocks in cuts:
        draws = jnp.exp(jax.random.uniform(jax.random.fold_in(own, dim), (blocks,), jnp.float32, smallest / len(cuts), high / len(cuts)))
        factor_of = factor_of * jnp.repeat(draws, shape[dim] // blocks).reshape([-1 if axis == dim else 1 for axis in range(len(shape))])
    return factor_of


def centred(own_key, dims, scale, limit, shards=(), kind=jnp.bfloat16):
    entries = jax.random.normal(own_key, dims, jnp.float32) * scale
    if len(shards) > 0:
        entries = steps_of(own_key, dims, shards, -0.22, 0.18) * entries
    return jnp.clip(entries, min=-limit, max=limit).astype(kind)


def setup_inputs(seed: int = 0) -> dict:
    key_of = jax.random.split(jax.random.key(seed), 13)
    q_attn = centred(key_of[0], (QUERIES, QLEN, D), 1.0, 6.0, ((0, 32), (2, 8)))
    q_resid = centred(key_of[1], (QUERIES, QLEN, D), 1.0, 6.0, ((0, 32), (2, 8)))
    p_attn = centred(key_of[2], (QUERIES, POSLEN, D), 1.0, 6.0, ((0, 32), (2, 8)))
    p_resid = centred(key_of[3], (QUERIES, POSLEN, D), 1.0, 6.0, ((0, 32), (2, 8)))
    w_out = centred(key_of[4], (D, D), D ** -0.5, 0.09375, ((0, 32), (1, 8)))
    w_snap = centred(key_of[5], (D, D), D ** -0.5, 0.09375, ((0, 32), (1, 8)))
    norm_gain = jnp.clip(jnp.exp(math.log(4.0) - 2.7725887 * jax.random.uniform(key_of[6], (D,), jnp.float32) ** steps_of(key_of[6], (D,), ((0, 8),), -0.2, 0.2)), 0.25, 4.0).astype(jnp.bfloat16)
    pass_attn = centred(key_of[7], (PASSAGES, PLEN, D), 1.0, 6.0, ((0, 32), (2, 8)))
    pass_resid = centred(key_of[8], (PASSAGES, PLEN, D), 1.0, 6.0, ((0, 32), (2, 8)))
    pass_len = draw_pass_len(jax.random.fold_in(key_of[12], 71), 0)
    block_owner = jax.random.permutation(key_of[10], BLOCKS).astype(jnp.int32)
    neg_ids = touch_ends(jax.random.randint(key_of[11], (QUERIES, NNEG), 0, PASSAGES), jax.random.fold_in(key_of[11], 1), 0, PASSAGES - 1).astype(jnp.int32)
    return dict(q_attn=q_attn, q_resid=q_resid, p_attn=p_attn, p_resid=p_resid, w_out=w_out, w_snap=w_snap, norm_gain=norm_gain, pass_attn=pass_attn, pass_resid=pass_resid, pass_len=pass_len, block_owner=block_owner, neg_ids=neg_ids)


EPS = 1e-06
TEMP = 0.05

def rms_rows(values):
    return values * lax.rsqrt(lax.optimization_barrier(jnp.mean(values * values, axis=-1, keepdims=True)) + EPS)

def token_forward(attn, resid, weight, gain):
    width = attn.shape[-1]
    flat_attn = attn.reshape(-1, width)
    hidden = resid.reshape(-1, width).astype(jnp.float32) + jnp.dot(flat_attn, weight, preferred_element_type=jnp.float32)
    factor = lax.rsqrt(lax.optimization_barrier(jnp.mean(hidden * hidden, axis=-1, keepdims=True)) + EPS)
    return (flat_attn, hidden, factor, hidden * factor * gain[None, :])

def contract_rows(left, right):
    return lax.dot_general(left, right, (((0,), (0,)), ((), ())), preferred_element_type=jnp.float32)

def seq_backward(pooled, grad, hidden, factor, gain, count):
    norm = lax.rsqrt(lax.optimization_barrier(jnp.mean(pooled * pooled, axis=-1, keepdims=True)) + EPS)
    emb = pooled * norm
    ge = norm * (grad - emb * lax.optimization_barrier(jnp.mean(emb * grad, axis=-1, keepdims=True)))
    seqs = pooled.shape[0]
    width = pooled.shape[1]
    upper = jnp.broadcast_to((ge / count * gain[None, :])[:, None, :], (seqs, count, width)).reshape(-1, width)
    normed = hidden * factor
    inner = lax.optimization_barrier(jnp.mean(normed * upper, axis=-1, keepdims=True))
    return (factor * (upper - normed * inner)).astype(jnp.bfloat16)

def reference(q_attn, q_resid, p_attn, p_resid, w_out, w_snap, norm_gain, pass_attn, pass_resid, pass_len, block_owner, neg_ids):
    hi = lax.Precision.HIGHEST
    gain = norm_gain.astype(jnp.float32)
    _, _, _, out_s = token_forward(pass_attn, pass_resid, w_snap, gain)
    out_s = out_s.reshape(PASSAGES, PLEN, D)
    mask = (jnp.arange(PLEN, dtype=jnp.int32)[None, :] < pass_len[:, None]).astype(jnp.float32)
    pooled_s = lax.optimization_barrier(jnp.sum(out_s * mask[:, :, None], axis=1)) / pass_len[:, None].astype(jnp.float32)
    passage_index = rms_rows(pooled_s).astype(jnp.bfloat16)
    flat_q, hidden_q, factor_q, out_q = token_forward(q_attn, q_resid, w_out, gain)
    flat_p, hidden_p, factor_p, out_p = token_forward(p_attn, p_resid, w_out, gain)
    pooled_q = lax.optimization_barrier(jnp.mean(out_q.reshape(QUERIES, QLEN, D), axis=1))
    pooled_p = lax.optimization_barrier(jnp.mean(out_p.reshape(QUERIES, POSLEN, D), axis=1))
    emb_q = rms_rows(pooled_q)
    emb_p = rms_rows(pooled_p)
    slots = block_owner[neg_ids // BLK] * BLK + neg_ids % BLK
    negs = passage_index[slots].astype(jnp.float32)
    scale = 1.0 / (D * TEMP)
    pos = lax.optimization_barrier(jnp.sum(emb_q * emb_p, axis=-1)) * scale
    neg = jnp.einsum('qc,qjc->qj', emb_q, negs, precision=hi) * scale
    exp_pos = jnp.exp(pos)
    exp_neg = jnp.exp(neg)
    total = exp_pos + lax.optimization_barrier(jnp.sum(exp_neg, axis=1))
    loss = jnp.mean(jnp.log(total) - pos)
    d_pos = exp_pos / total - 1.0
    d_neg = exp_neg / total[:, None]
    grad_q = (d_pos[:, None] * emb_p + jnp.einsum('qj,qjc->qc', d_neg, negs, precision=hi)) * scale
    grad_p = d_pos[:, None] * emb_q * scale
    dh_q = seq_backward(pooled_q, grad_q, hidden_q, factor_q, gain, QLEN)
    dh_p = seq_backward(pooled_p, grad_p, hidden_p, factor_p, gain, POSLEN)
    w_grad = contract_rows(flat_q, dh_q) + contract_rows(flat_p, dh_p)
    return (loss, w_grad, passage_index)
```

```python
import functools

import jax
import jax.numpy as jnp
from jax import lax
from jax.experimental import pallas as pl
from jax.experimental.pallas import tpu as pltpu
from jax.sharding import PartitionSpec as P

EPS = 1e-06
TEMP = 0.05
WIDTH = 4096
COLS = 512
STOK = 512
ETOK = 384
SCALE = 1.0 / (WIDTH * TEMP)
MESH = pl.DeviceIdType.MESH
HI = lax.Precision.HIGHEST
F32 = jnp.float32
BF16 = jnp.bfloat16
HALF = (0, 1, 1, 0, 0, 1)
STEP = (1, 1, -1, -1, 1, -1)


def lanes4(col):
    return jnp.concatenate([col, col, col, col], axis=1)


def spread_rows(row):
    return jnp.broadcast_to(row, (128, 128)).T


def square_rows(h_ref, block):
    part = h_ref[pl.ds(block * 128, 128), :]
    part = part * part
    part = (part[:, 0:128] + part[:, 128:256]) + (part[:, 256:384] + part[:, 384:512])
    return jnp.sum(part.T, axis=0, keepdims=True)


def kernel(
    q_attn, q_resid, p_attn, p_resid, w_out, w_snap, gain_ref, s_attn, s_resid,
    pass_len, block_owner, neg_ids,
    loss_ref, grad_ref, index_ref,
    a_s, a_e, w_s, w_o, r_s, r_e, h_s, h_e, a_t,
    ar_s, ar_p, ar_e, ar_g, ig, pool_s, vec, vec_g, s_full, fcol, gcol, f_row, urow, dh,
    own, psend, precv, xsend, xrecv, zsend, zrecv, l_c, l_x, l_z,
    loc, y_ss, y_rs, z_ss, z_rs, wz_ss, wz_rs, wx_ss, wx_rs, wc_ss, wc_rs,
    ar_ss, ar_rs, ig_ss, ig_rs, pc_ss, pc_rs, px_ss, px_rs, pz_ss, pz_rs, ls_ss, ls_rs,
):
    grp = lax.axis_index("grp")
    t = lax.axis_index("tp")
    core = grp % 2
    x = (grp // 2) % 4
    lo = grp // 8
    y = t // 2
    hi = t % 2
    t_far = y * 2 + (1 - hi)

    def grp_of(l_, x_, c_):
        return (l_ * 8 + x_ * 2 + c_, t)

    def tp_of(y_, h_):
        return (grp, y_ * 2 + h_)

    def remote(src, dst, ss, rs, device):
        return pltpu.make_async_remote_copy(
            src_ref=src, dst_ref=dst, send_sem=ss, recv_sem=rs, device_id=device,
            device_id_type=MESH,
        )

    locals_ = [
        pltpu.make_async_copy(w_snap, w_s.at[grp], loc.at[0]),
        pltpu.make_async_copy(s_attn, a_s.at[t], loc.at[1]),
        pltpu.make_async_copy(w_out, w_o.at[grp], loc.at[2]),
        pltpu.make_async_copy(q_attn, a_e.at[t, pl.ds(0, 128)], loc.at[3]),
        pltpu.make_async_copy(p_attn, a_e.at[t, pl.ds(128, 256)], loc.at[4]),
        pltpu.make_async_copy(s_resid, r_s, loc.at[5]),
        pltpu.make_async_copy(q_resid, r_e.at[pl.ds(0, 128)], loc.at[6]),
        pltpu.make_async_copy(p_resid, r_e.at[pl.ds(128, 256)], loc.at[7]),
    ]
    for copy in locals_:
        copy.start()

    barrier = pltpu.get_barrier_semaphore()
    peers = [grp_of(lo, x, 1 - core)]
    for d in (1, 2, 3):
        peers.append(grp_of(lo, (x + d) % 4, core))
        peers.append(grp_of((lo + d) % 4, x, core))
    for j in range(1, 8):
        peers.append(tp_of((y + j // 2) % 4, (hi + j % 2) % 2))
    for peer in peers:
        pl.semaphore_signal(barrier, inc=1, device_id=peer, device_id_type=MESH)
    vec[...] = jnp.zeros_like(vec)
    s_full[...] = jnp.zeros_like(s_full)
    pl.semaphore_wait(barrier, len(peers))

    def y_copy(k, i):
        buf, size = ((a_s, 256), (a_e, 192))[k % 2]
        half_of = hi if k < 2 else 1 - hi
        row = y if i < 4 else (y - STEP[i] + 4) % 4
        ref = buf.at[row * 2 + half_of, pl.ds(HALF[i] * size, size)]
        return remote(
            ref, ref, y_ss.at[k, i], y_rs.at[k, i], tp_of((y + STEP[i] + 4) % 4, hi)
        )

    def y_arrival(k, i):
        buf, size = ((a_s, 256), (a_e, 192))[k % 2]
        half_of = hi if k < 2 else 1 - hi
        row = (y - STEP[i] * (1 if i < 4 else 2) + 4) % 4
        ref = buf.at[row * 2 + half_of, pl.ds(HALF[i] * size, size)]
        return remote(ref, ref, y_ss.at[k, i], y_rs.at[k, i], tp_of(y, hi))

    def far_copy(k, half, slot):
        buf, size = ((a_s, 256), (a_e, 192))[k]
        ref = buf.at[slot, pl.ds(half * size, size)]
        return remote(ref, ref, z_ss.at[k, half], z_rs.at[k, half], tp_of(y, 1 - hi))

    weights = (w_s, w_o)

    def wz_copy(m, d, source):
        ref = weights[m].at[source * 8 + x * 2 + core]
        return remote(
            ref, ref, wz_ss.at[m, d], wz_rs.at[m, d], grp_of((lo + d) % 4, x, core)
        )

    def wx_copy(m, b, d, x_):
        ref = weights[m].at[((lo - b + 4) % 4) * 8 + x_ * 2 + core]
        return remote(
            ref, ref, wx_ss.at[m, b, d], wx_rs.at[m, b, d], grp_of(lo, (x + d) % 4, core)
        )

    def wc_copy(m, b, d, c_):
        ref = weights[m].at[((lo - b + 4) % 4) * 8 + ((x - d + 4) % 4) * 2 + c_]
        return remote(
            ref, ref, wc_ss.at[m, b, d], wc_rs.at[m, b, d], grp_of(lo, x, 1 - core)
        )

    def w_spread(m, b):
        for d in (2, 1, 3):
            wx_copy(m, b, d, x).start()
        wc_copy(m, b, 0, core).start()

    def ar_copy(which, buf, j, slot):
        ref = buf.at[slot]
        return remote(
            ref, ref, ar_ss.at[which, j], ar_rs.at[which, j],
            tp_of((y + j // 2) % 4, (hi + j % 2) % 2),
        )

    def ar_start(which, buf):
        for j in (5, 7, 3, 4, 1, 2, 6):
            ar_copy(which, buf, j, t).start()

    def ar_finish(which, buf):
        for j in range(1, 8):
            ar_copy(which, buf, j, ((y - j // 2 + 4) % 4) * 2 + (hi + j % 2) % 2).wait_recv()
        total = buf[0]
        for j in range(1, 8):
            total = total + buf[j]
        return total

    def ig_copy(i, l_, x_, c_):
        if i == 0:
            ref, device = ig.at[lo, x * 2 + c_], grp_of(lo, x, 1 - core)
        elif i < 4:
            ref, device = ig.at[lo, pl.ds(x_ * 2, 2)], grp_of(lo, (x + i) % 4, core)
        else:
            ref, device = ig.at[l_], grp_of((lo + i - 3) % 4, x, core)
        return remote(ref, ref, ig_ss.at[i], ig_rs.at[i], device)

    def multiply(h_ref, buf, w_ref, half_of):
        def body(i, carry):
            k = ((y + i) % 4) * 2 + half_of
            piece = w_ref[pl.ds(4 * k, 4)].reshape(512, COLS)
            h_ref[...] += jnp.dot(buf[k], piece, preferred_element_type=F32)
            return carry

        lax.fori_loop(0, 4, body, 0)

    def turn(half_of):
        def body(i, carry):
            k = ((y + i) % 4) * 2 + half_of
            a_t[pl.ds(k * 512, 512), :] = a_e[k].T
            return carry

        lax.fori_loop(0, 4, body, 0)

    for i in (0, 1):
        locals_[i].wait()
    for d in (2, 1, 3):
        wz_copy(0, d, lo).start()
    w_spread(0, 0)
    for i in range(4):
        y_copy(0, i).start()
    for half in (0, 1):
        far_copy(0, half, t).start()
    for i in (2, 3, 4):
        locals_[i].wait()
    for d in (2, 1, 3):
        wz_copy(1, d, lo).start()
    w_spread(1, 0)
    for i in range(4):
        y_copy(1, i).start()
    for half in (0, 1):
        far_copy(1, half, t).start()
    for i in (5, 6, 7):
        locals_[i].wait()
    h_s[...] = r_s[...].astype(F32)
    h_e[...] = r_e[...].astype(F32)

    for b in (1, 3, 2):
        wz_copy(0, b, (lo - b + 4) % 4).wait_recv()
        w_spread(0, b)
    for i in (0, 2):
        y_arrival(0, i).wait_recv()
        y_copy(0, 4 + i // 2).start()
    for b in (1, 3, 2):
        wz_copy(1, b, (lo - b + 4) % 4).wait_recv()
        w_spread(1, b)
    for i in (0, 2):
        y_arrival(1, i).wait_recv()
        y_copy(1, 4 + i // 2).start()
    for half in (0, 1):
        far_copy(0, half, t_far).wait_recv()
    for i in range(4):
        y_copy(2, i).start()
    for b in (0, 1, 3, 2):
        for d in (1, 3, 2):
            wx_copy(0, b, d, (x - d + 4) % 4).wait_recv()
            wc_copy(0, b, d, core).start()
    for i in (0, 2):
        y_arrival(2, i).wait_recv()
        y_copy(2, 4 + i // 2).start()
    for b in range(4):
        for d in range(4):
            wc_copy(0, b, d, 1 - core).wait_recv()
    for i in (1, 3, 4, 5):
        y_arrival(0, i).wait_recv()
    multiply(h_s, a_s, w_s, hi)
    for half in (0, 1):
        far_copy(1, half, t_far).wait_recv()
    for i in range(4):
        y_copy(3, i).start()
    for i in (1, 3, 4, 5):
        y_arrival(1, i).wait_recv()
    turn(hi)
    for b in (0, 1, 3, 2):
        for d in (1, 3, 2):
            wx_copy(1, b, d, (x - d + 4) % 4).wait_recv()
            wc_copy(1, b, d, core).start()
    for i in (1, 3, 4, 5):
        y_arrival(2, i).wait_recv()
    multiply(h_s, a_s, w_s, 1 - hi)

    ar_s[t] = jnp.zeros((8, 128), F32)
    for b in range(4):
        ar_s[t, b : b + 1, :] = square_rows(h_s, b)
    ar_start(0, ar_s)
    for i in (0, 2):
        y_arrival(3, i).wait_recv()
        y_copy(3, 4 + i // 2).start()
    for b in range(4):
        for d in range(4):
            wc_copy(1, b, d, 1 - core).wait_recv()
    multiply(h_e, a_e, w_o, hi)
    gain = gain_ref[...].astype(F32)

    factor_s = lax.rsqrt(ar_finish(0, ar_s) / WIDTH + EPS)
    ar_p[t] = jnp.zeros((8, 128), F32)
    for s in range(2):
        count = pass_len[s]
        total = jnp.zeros((1, COLS), F32)
        for b in range(2):
            rows = lax.broadcasted_iota(jnp.int32, (128, 128), 0) + b * 128
            col = spread_rows(factor_s[2 * s + b : 2 * s + b + 1, :])
            col = jnp.where(rows < count, col, 0.0)
            part = h_s[pl.ds((2 * s + b) * 128, 128), :] * lanes4(col)
            total = total + jnp.sum(part, axis=0, keepdims=True)
        total = total * gain / jnp.full((1, COLS), count, jnp.int32).astype(F32)
        pool_s[s : s + 1, :] = total
        square = jnp.sum(total * total, axis=1, keepdims=True)
        ar_p[t, s : s + 1, :] = jnp.broadcast_to(square, (1, 128))
    ar_start(1, ar_p)
    norm_s = lax.rsqrt(ar_finish(1, ar_p) / WIDTH + EPS)
    for s in range(2):
        row = (pool_s[s : s + 1, :] * lanes4(norm_s[s : s + 1, :])).astype(BF16).astype(F32)
        pool_s[s : s + 1, :] = row
        for b in range(4):
            ig[lo, x * 2 + core, 4 * s + b : 4 * s + b + 1, :] = row[:, b * 128 : b * 128 + 128]
    index_ref[...] = pool_s[0:2, :].astype(BF16)
    ig_copy(0, lo, x, core).start()
    ig_copy(0, lo, x, 1 - core).wait_recv()
    for i in (2, 1, 3):
        ig_copy(i, lo, x, core).start()

    for i in (1, 3, 4, 5):
        y_arrival(3, i).wait_recv()
    multiply(h_e, a_e, w_o, 1 - hi)
    ar_e[t] = jnp.zeros((8, 128), F32)
    for b in range(3):
        ar_e[t, b : b + 1, :] = square_rows(h_e, b)
    ar_start(2, ar_e)
    for i in (1, 2, 3):
        ig_copy(i, lo, (x - i + 4) % 4, core).wait_recv()
    for i in (5, 4, 6):
        ig_copy(i, lo, x, core).start()
    turn(1 - hi)

    factor = lax.rsqrt(ar_finish(2, ar_e) / WIDTH + EPS)
    f_row[...] = factor
    for b in range(3):
        fcol[pl.ds(b * 128, 128), :] = spread_rows(factor[b : b + 1, :])
    for r, (first, count) in enumerate(((0, 64), (64, 64), (128, 128), (256, 128))):
        part = h_e[pl.ds(first, count), :] * lanes4(fcol[pl.ds(first, count), :])
        vec[r : r + 1, :] = jnp.sum(part, axis=0, keepdims=True) * gain / count
    for i in (4, 5, 6):
        ig_copy(i, (lo - i + 3 + 4) % 4, x, core).wait_recv()
    for r in range(2):
        for j in range(8):
            name = neg_ids[r, j]
            owner = block_owner[name // 2]
            tile = ig[owner // 8, owner % 8]
            piece = jnp.where(name % 2 == 0, tile[0:4, :], tile[4:8, :])
            at = 8 + 8 * r + j
            for b in range(4):
                vec[at : at + 1, b * 128 : b * 128 + 128] = piece[b : b + 1, :]

    nt = (((1,), (1,)), ((), ()))
    vec_g[...] = vec[0:32, :] * gain
    sims = lax.dot_general(vec_g[...], h_e[...], nt, precision=HI, preferred_element_type=F32)
    gram = lax.dot_general(vec[0:8, :], vec[...], nt, precision=HI, preferred_element_type=F32)
    first = lax.broadcasted_iota(jnp.int32, (1, 128), 1) < 64
    ar_g[t, 0:8, :] = jnp.where(first, sims[8:16, 0:128], sims[16:24, 0:128])
    ar_g[t, 8:16, :] = jnp.zeros((8, 128), F32)
    ar_g[t, 8:9, :] = jnp.where(first, sims[0:1, 0:128], sims[1:2, 0:128])
    ar_g[t, 9:10, :] = jnp.where(first, sims[2:3, 0:128], sims[3:4, 0:128])
    ar_g[t, 10:11, :] = sims[0:1, 128:256]
    ar_g[t, 11:12, :] = sims[2:3, 128:256]
    ar_g[t, 12:13, :] = sims[1:2, 256:384]
    ar_g[t, 13:14, :] = sims[3:4, 256:384]
    ar_g[t, 16:24, :] = gram
    ar_start(3, ar_g)
    both = ar_finish(3, ar_g)

    gram = both[16:24, :]
    row = lax.broadcasted_iota(jnp.int32, (8, 128), 0)
    lane = lax.broadcasted_iota(jnp.int32, (8, 128), 1)
    diag = jnp.where((lane == row) & (row < 4), gram, 0.0)
    norm_row = lax.rsqrt(jnp.sum(diag, axis=1, keepdims=True) / WIDTH + EPS)
    norm_lane = lax.rsqrt(jnp.sum(diag, axis=0, keepdims=True) / WIDTH + EPS)
    norm_lane = jnp.where(lane < 4, norm_lane, 1.0)
    unit = gram * norm_row * norm_lane
    is_pos = (lane == row + 2) & (row < 2)
    is_neg = (lane >= 8 + 8 * row) & (lane < 16 + 8 * row) & (row < 2)
    pos = jnp.sum(jnp.where(is_pos, unit, 0.0), axis=1, keepdims=True) * SCALE
    exp_neg = jnp.where(is_neg, jnp.exp(jnp.where(is_neg, unit, 0.0) * SCALE), 0.0)
    exp_pos = jnp.exp(pos)
    total = exp_pos + jnp.sum(exp_neg, axis=1, keepdims=True)
    terms = jnp.where(row < 2, jnp.log(total) - pos, 0.0)
    loss = jnp.sum(terms, axis=0, keepdims=True)
    d_pos = jnp.where(is_pos, exp_pos / total - 1.0, 0.0)
    pos_lane = jnp.sum(d_pos, axis=0, keepdims=True)
    pos_row = jnp.sum(jnp.where(lane == row, pos_lane, 0.0), axis=1, keepdims=True)
    coef = d_pos + exp_neg / total
    coef = coef + jnp.where((lane == row - 2) & (row < 4), pos_row, 0.0)
    coef = coef * SCALE
    back = jnp.sum(coef * unit, axis=1, keepdims=True) / WIDTH
    coef = norm_row * (coef * norm_lane - jnp.where(lane == row, back * norm_row, 0.0))
    coef = jnp.where(row < 4, coef, 0.0)
    coef = coef / jnp.where(row < 2, 64.0, 128.0)

    l_c[core] = jnp.broadcast_to(loss, (8, 128))
    pair_loss = remote(
        l_c.at[core], l_c.at[core], ls_ss.at[0], ls_rs.at[0], grp_of(lo, x, 1 - core)
    )
    pair_loss.start()

    s_full[8:16, 0:128] = both[0:8, :]
    s_full[16:24, 0:128] = both[0:8, :]
    s_full[0:2, 0:128] = jnp.broadcast_to(both[8:9, :], (2, 128))
    s_full[2:4, 0:128] = jnp.broadcast_to(both[9:10, :], (2, 128))
    s_full[0:1, 128:256] = both[10:11, :]
    s_full[2:3, 128:256] = both[11:12, :]
    s_full[1:2, 256:384] = both[12:13, :]
    s_full[3:4, 256:384] = both[13:14, :]
    inner = jnp.dot(coef, s_full[...], precision=HI, preferred_element_type=F32)
    urow[...] = jnp.dot(coef, vec[...], precision=HI, preferred_element_type=F32) * gain
    wanted = (
        ((row == 0) & (lane < 64)) | ((row == 1) & (lane >= 64)),
        row == 2,
        row == 3,
    )
    for b in range(3):
        line = jnp.sum(
            jnp.where(wanted[b], inner[:, b * 128 : b * 128 + 128], 0.0), axis=0, keepdims=True
        )
        f = f_row[b : b + 1, :]
        gcol[pl.ds(b * 128, 128), :] = spread_rows(line * f * f / WIDTH)
    for r, (first, count) in enumerate(((0, 64), (64, 64), (128, 128), (256, 128))):
        at = pl.ds(first, count)
        part = urow[r : r + 1, :] - h_e[at, :] * lanes4(gcol[at, :])
        dh[at, :] = (lanes4(fcol[at, :]) * part).astype(BF16)

    def pc_copy(i, x_):
        return remote(
            psend.at[x_], precv.at[x_], pc_ss.at[i], pc_rs.at[i], grp_of(lo, x, 1 - core)
        )

    def px_copy(i, d, dst):
        return remote(
            xsend.at[i, d], xrecv.at[i, d], px_ss.at[i, d], px_rs.at[i, d], grp_of(lo, dst, core)
        )

    def pz_copy(d):
        return remote(
            zsend.at[d], zrecv.at[d], pz_ss.at[d], pz_rs.at[d], grp_of((lo + d) % 4, x, core)
        )

    turns = (2, 1, 3, 0)
    for i in range(4):
        x_ = (x + turns[i]) % 4

        def other(l_, carry, x_=x_):
            at = pl.ds((l_ * 8 + x_ * 2 + 1 - core) * 128, 128)
            psend[x_, l_] = jnp.dot(
                a_t[at, :], dh[...], preferred_element_type=F32
            ).astype(BF16)
            return carry

        def mine(l_, carry, x_=x_):
            at = pl.ds((l_ * 8 + x_ * 2 + core) * 128, 128)
            own[x_, l_] = jnp.dot(a_t[at, :], dh[...], preferred_element_type=F32)
            return carry

        lax.fori_loop(0, 4, other, 0)
        pc_copy(i, x_).start()
        lax.fori_loop(0, 4, mine, 0)

    pair_loss.wait_recv()
    l_x[x] = l_c[0] + l_c[1]

    def lx_copy(d, slot):
        return remote(
            l_x.at[slot], l_x.at[slot], ls_ss.at[d], ls_rs.at[d], grp_of(lo, (x + d) % 4, core)
        )

    def lz_copy(d, slot):
        return remote(
            l_z.at[slot], l_z.at[slot], ls_ss.at[3 + d], ls_rs.at[3 + d],
            grp_of((lo + d) % 4, x, core),
        )

    for d in (1, 2, 3):
        lx_copy(d, x).start()
    for i in range(3):
        x_ = (x + turns[i]) % 4
        pc_copy(i, x_).wait_recv()
        for d in (2, 1, 3, 0):
            l_ = (lo + d) % 4
            xsend[i, d] = (own[x_, l_] + precv[x_, l_].astype(F32)).astype(BF16)
            px_copy(i, d, x_).start()
    pc_copy(3, x).wait_recv()
    for d in (1, 2, 3):
        lx_copy(d, (x - d + 4) % 4).wait_recv()
    l_z[lo] = (l_x[0] + l_x[1]) + (l_x[2] + l_x[3])
    for d in (1, 2, 3):
        lz_copy(d, lo).start()
    for d in (2, 1, 3, 0):
        l_ = (lo + d) % 4
        total = own[x, l_] + precv[x, l_].astype(F32)
        for i in (1, 2, 0):
            px_copy(i, d, x).wait_recv()
        total = total + (xrecv[0, d].astype(F32) + xrecv[1, d].astype(F32) + xrecv[2, d].astype(F32))
        if d == 0:
            grad_ref[...] = total
        else:
            zsend[d] = total.astype(BF16)
            pz_copy(d).start()
    for d in (1, 2, 3):
        lz_copy(d, (lo - d + 4) % 4).wait_recv()
    loss_ref[...] = ((l_z[0] + l_z[1]) + (l_z[2] + l_z[3]))[0:1, 0:1] / 64.0
    for d in (1, 3, 2):
        pz_copy(d).wait_recv()
    grad_ref[...] += (zrecv[1].astype(F32) + zrecv[2].astype(F32)) + zrecv[3].astype(F32)

    for k in range(4):
        for i in range(6):
            y_copy(k, i).wait_send()
    for k in range(2):
        for half in (0, 1):
            far_copy(k, half, t).wait_send()
        for d in (1, 2, 3):
            wz_copy(k, d, lo).wait_send()
        for b in range(4):
            for d in (1, 2, 3):
                wx_copy(k, b, d, x).wait_send()
            for d in range(4):
                wc_copy(k, b, d, core).wait_send()
    for which, buf in enumerate((ar_s, ar_p, ar_e, ar_g)):
        for j in range(1, 8):
            ar_copy(which, buf, j, t).wait_send()
    for i in range(7):
        ig_copy(i, lo, x, core).wait_send()
    pair_loss.wait_send()
    for d in (1, 2, 3):
        lx_copy(d, x).wait_send()
        lz_copy(d, lo).wait_send()
        pz_copy(d).wait_send()
    for i in range(4):
        pc_copy(i, x).wait_send()
    for i in range(3):
        for d in range(4):
            px_copy(i, d, x).wait_send()


def shards(
    q_attn, q_resid, p_attn, p_resid, w_out, w_snap, norm_gain, pass_attn, pass_resid,
    pass_len, block_owner, neg_ids,
):
    hbm = pl.BlockSpec(memory_space=pl.ANY)
    vmem = pl.BlockSpec(memory_space=pltpu.VMEM)
    smem = pl.BlockSpec(memory_space=pltpu.SMEM)
    dma = pltpu.SemaphoreType.DMA
    loss, grad, index = pl.pallas_call(
        kernel,
        out_shape=(
            jax.ShapeDtypeStruct((1, 1), F32),
            jax.ShapeDtypeStruct((128, COLS), F32),
            jax.ShapeDtypeStruct((2, COLS), BF16),
        ),
        in_specs=[hbm] * 6 + [vmem] + [hbm] * 2 + [smem] * 3,
        out_specs=(vmem, vmem, vmem),
        scratch_shapes=[
            pltpu.VMEM((8, STOK, COLS), BF16),
            pltpu.VMEM((8, ETOK, COLS), BF16),
            pltpu.VMEM((32, 128, COLS), BF16),
            pltpu.VMEM((32, 128, COLS), BF16),
            pltpu.VMEM((STOK, COLS), BF16),
            pltpu.VMEM((ETOK, COLS), BF16),
            pltpu.VMEM((STOK, COLS), F32),
            pltpu.VMEM((ETOK, COLS), F32),
            pltpu.VMEM((WIDTH, ETOK), BF16),
            pltpu.VMEM((8, 8, 128), F32),
            pltpu.VMEM((8, 8, 128), F32),
            pltpu.VMEM((8, 8, 128), F32),
            pltpu.VMEM((8, 24, 128), F32),
            pltpu.VMEM((4, 8, 8, 128), F32),
            pltpu.VMEM((8, COLS), F32),
            pltpu.VMEM((128, COLS), F32),
            pltpu.VMEM((32, COLS), F32),
            pltpu.VMEM((128, ETOK), F32),
            pltpu.VMEM((ETOK, 128), F32),
            pltpu.VMEM((ETOK, 128), F32),
            pltpu.VMEM((8, 128), F32),
            pltpu.VMEM((8, COLS), F32),
            pltpu.VMEM((ETOK, COLS), BF16),
            pltpu.VMEM((4, 4, 128, COLS), F32),
            pltpu.VMEM((4, 4, 128, COLS), BF16),
            pltpu.VMEM((4, 4, 128, COLS), BF16),
            pltpu.VMEM((3, 4, 128, COLS), BF16),
            pltpu.VMEM((3, 4, 128, COLS), BF16),
            pltpu.VMEM((4, 128, COLS), BF16),
            pltpu.VMEM((4, 128, COLS), BF16),
            pltpu.VMEM((2, 8, 128), F32),
            pltpu.VMEM((4, 8, 128), F32),
            pltpu.VMEM((4, 8, 128), F32),
            dma((8,)),
            dma((4, 6)), dma((4, 6)),
            dma((2, 2)), dma((2, 2)),
            dma((2, 4)), dma((2, 4)),
            dma((2, 4, 4)), dma((2, 4, 4)),
            dma((2, 4, 4)), dma((2, 4, 4)),
            dma((4, 8)), dma((4, 8)),
            dma((7,)), dma((7,)),
            dma((4,)), dma((4,)),
            dma((3, 4)), dma((3, 4)),
            dma((4,)), dma((4,)),
            dma((7,)), dma((7,)),
        ],
        compiler_params=pltpu.CompilerParams(
            collective_id=0, has_side_effects=True, vmem_limit_bytes=56 * 2**20
        ),
    )(
        q_attn.reshape(128, COLS),
        q_resid.reshape(128, COLS),
        p_attn.reshape(256, COLS),
        p_resid.reshape(256, COLS),
        w_out,
        w_snap,
        norm_gain.reshape(1, COLS),
        pass_attn.reshape(STOK, COLS),
        pass_resid.reshape(STOK, COLS),
        pass_len,
        block_owner,
        neg_ids,
    )
    return (loss[0, 0], grad, index)


def solution(mesh):
    placed = (
        P("grp", None, "tp"),
        P("grp", None, "tp"),
        P("grp", None, "tp"),
        P("grp", None, "tp"),
        P("grp", "tp"),
        P("grp", "tp"),
        P("tp"),
        P("grp", None, "tp"),
        P("grp", None, "tp"),
        P("grp"),
        P(),
        P("grp", None),
    )
    return jax.shard_map(
        shards,
        mesh=mesh,
        in_specs=placed,
        out_specs=(P(), P("grp", "tp"), P("grp", "tp")),
        check_vma=False,
    )
```

```python
import functools

import jax
import jax.numpy as jnp
from jax import lax
from jax.experimental import pallas as pl
from jax.experimental.pallas import tpu as pltpu
from jax.sharding import PartitionSpec as P

EPS = 1e-06
TEMP = 0.05
WIDTH = 4096
COLS = 512
STOK = 512
ETOK = 384
SCALE = 1.0 / (WIDTH * TEMP)
MESH = pl.DeviceIdType.MESH
HI = lax.Precision.HIGHEST
F32 = jnp.float32
BF16 = jnp.bfloat16
HALF = (0, 1, 1, 0, 0, 1)
STEP = (1, 1, -1, -1, 1, -1)


class Copy:
    def __init__(self, sent, src, dst, sems, at, device):
        self.sent = sent
        self.key = (id(sems), at)
        self.copy = pltpu.make_async_remote_copy(
            src_ref=src, dst_ref=dst, send_sem=sems[0].at[at], recv_sem=sems[1].at[at],
            device_id=device, device_id_type=MESH,
        )

    def start(self, when=None):
        self.when = when
        self.sent.append(self)
        self.guard(when, self.copy.start)

    def wait_recv(self, when=None):
        self.guard(when, self.copy.wait_recv)

    def wait_send(self):
        self.guard(self.when, self.copy.wait_send)

    def guard(self, when, action):
        if when is None:
            action()
        else:
            pl.when(when)(action)


def lanes4(col):
    return jnp.concatenate([col, col, col, col], axis=1)


def spread_rows(row):
    return jnp.broadcast_to(row, (128, 128)).T


def square_rows(h_ref, block):
    part = h_ref[pl.ds(block * 128, 128), :]
    part = part * part
    part = (part[:, 0:128] + part[:, 128:256]) + (part[:, 256:384] + part[:, 384:512])
    return jnp.sum(part.T, axis=0, keepdims=True)


def kernel(
    q_attn, q_resid, p_attn, p_resid, w_out, w_snap, gain_ref, s_attn, s_resid,
    pass_len, block_owner, neg_ids,
    loss_ref, grad_ref, index_ref,
    a_s, a_e, w_s, w_o, r_s, r_e, h_s, h_e, a_t,
    ar_s, ar_p, ar_e, ar_g, ig, pool_s, vec, vec_g, s_full, fcol, gcol, f_row, urow, dh,
    own, psend, precv, xsend, xrecv, zsend, zrecv, l_c, l_x, l_z,
    loc, y_sems, z_sems, wz_sems, wx_sems, wc_sems, ar_sems, ig_sems, pc_sems, px_sems, pz_sems,
    ls_sems,
):
    grp = lax.axis_index("grp")
    t = lax.axis_index("tp")
    core = grp % 2
    x = (grp // 2) % 4
    lo = grp // 8
    y = t // 2
    hi = t % 2
    t_far = y * 2 + (1 - hi)

    def grp_of(l_, x_, c_):
        return (l_ * 8 + x_ * 2 + c_, t)

    def tp_of(y_, h_):
        return (grp, y_ * 2 + h_)

    sent = []

    def remote(src, dst, sems, at, device):
        return Copy(sent, src, dst, sems, at, device)

    locals_ = [
        pltpu.make_async_copy(w_snap, w_s.at[grp], loc.at[0]),
        pltpu.make_async_copy(s_attn, a_s.at[t], loc.at[1]),
        pltpu.make_async_copy(w_out, w_o.at[grp], loc.at[2]),
        pltpu.make_async_copy(q_attn, a_e.at[t, pl.ds(0, 128)], loc.at[3]),
        pltpu.make_async_copy(p_attn, a_e.at[t, pl.ds(128, 256)], loc.at[4]),
        pltpu.make_async_copy(s_resid, r_s, loc.at[5]),
        pltpu.make_async_copy(q_resid, r_e.at[pl.ds(0, 128)], loc.at[6]),
        pltpu.make_async_copy(p_resid, r_e.at[pl.ds(128, 256)], loc.at[7]),
    ]
    for copy in locals_:
        copy.start()

    barrier = pltpu.get_barrier_semaphore()
    peers = [grp_of(lo, x, 1 - core)]
    for d in (1, 2, 3):
        peers.append(grp_of(lo, (x + d) % 4, core))
        peers.append(grp_of((lo + d) % 4, x, core))
        peers.append(tp_of((y + d) % 4, hi))
    peers.append(tp_of(y, 1 - hi))
    for peer in peers:
        pl.semaphore_signal(barrier, inc=1, device_id=peer, device_id_type=MESH)
    vec[...] = jnp.zeros_like(vec)
    s_full[...] = jnp.zeros_like(s_full)
    pl.semaphore_wait(barrier, len(peers))

    def y_copy(k, i):
        buf, size = ((a_s, 256), (a_e, 192))[k % 2]
        half_of = hi if k < 2 else 1 - hi
        row = y if i < 4 else (y - STEP[i] + 4) % 4
        ref = buf.at[row * 2 + half_of, pl.ds(HALF[i] * size, size)]
        return remote(
            ref, ref, y_sems, (k, i), tp_of((y + STEP[i] + 4) % 4, hi)
        )

    def y_arrival(k, i):
        buf, size = ((a_s, 256), (a_e, 192))[k % 2]
        half_of = hi if k < 2 else 1 - hi
        row = (y - STEP[i] * (1 if i < 4 else 2) + 4) % 4
        ref = buf.at[row * 2 + half_of, pl.ds(HALF[i] * size, size)]
        return remote(ref, ref, y_sems, (k, i), tp_of(y, hi))

    def far_copy(k, half, slot):
        buf, size = ((a_s, 256), (a_e, 192))[k]
        ref = buf.at[slot, pl.ds(half * size, size)]
        return remote(ref, ref, z_sems, (k, half), tp_of(y, 1 - hi))

    weights = (w_s, w_o)

    def wz_copy(m, way, step, source):
        ref = weights[m].at[source * 8 + x * 2 + core]
        return remote(
            ref, ref, wz_sems, (m, way, step),
            grp_of((lo + (1, 3)[way]) % 4, x, core),
        )

    def wz_first(m):
        wz_copy(m, 0, 0, lo).start(lo < 3)
        wz_copy(m, 1, 0, lo).start(lo > 0)

    def wz_step(m, step):
        for way in (0, 1):
            source = (lo + (step + 1) * (-1, 1)[way] + 4) % 4
            came = (lo > step, lo < 3 - step)[way]
            wz_copy(m, way, step, source).wait_recv(came)
            if step < 2:
                wz_copy(m, way, step + 1, source).start(came & (lo < 3, lo > 0)[way])
            for d in (2, 1, 3):
                wx_copy(m, 1 + 3 * way + step, d, x).start(came)
            wc_copy(m, 1 + 3 * way + step, 0, core).start(came)

    def line(b):
        if b == 0:
            return lo, None
        step = (b - 1) % 3
        way = (b - 1) // 3
        return (lo + (step + 1) * (-1, 1)[way] + 4) % 4, (lo > step, lo < 3 - step)[way]

    def w_pass(m, b):
        for d in (1, 3, 2):
            wx_copy(m, b, d, (x - d + 4) % 4).wait_recv(line(b)[1])
            wc_copy(m, b, d, core).start(line(b)[1])

    def w_done(m):
        for b in range(7):
            for d in range(4):
                wc_copy(m, b, d, 1 - core).wait_recv(line(b)[1])

    def wx_copy(m, b, d, x_):
        ref = weights[m].at[line(b)[0] * 8 + x_ * 2 + core]
        return remote(
            ref, ref, wx_sems, (m, b, d), grp_of(lo, (x + d) % 4, core)
        )

    def wc_copy(m, b, d, c_):
        ref = weights[m].at[line(b)[0] * 8 + ((x - d + 4) % 4) * 2 + c_]
        return remote(
            ref, ref, wc_sems, (m, b, d), grp_of(lo, x, 1 - core)
        )

    def w_spread(m, b):
        for d in (2, 1, 3):
            wx_copy(m, b, d, x).start()
        wc_copy(m, b, 0, core).start()

    def ar_copy(which, buf, j, slot):
        ref = buf.at[slot]
        return remote(
            ref, ref, ar_sems, (which, j),
            tp_of((y + j // 2) % 4, (hi + j % 2) % 2),
        )

    def ar_start(which, buf):
        for j in (5, 7, 3, 4, 1, 2, 6):
            ar_copy(which, buf, j, t).start()

    def ar_finish(which, buf):
        for j in range(1, 8):
            ar_copy(which, buf, j, ((y - j // 2 + 4) % 4) * 2 + (hi + j % 2) % 2).wait_recv()
        total = buf[0]
        for j in range(1, 8):
            total = total + buf[j]
        return total

    def ig_copy(i, l_, x_, c_):
        if i == 0:
            ref, device = ig.at[lo, x * 2 + c_], grp_of(lo, x, 1 - core)
        elif i < 4:
            ref, device = ig.at[lo, pl.ds(x_ * 2, 2)], grp_of(lo, (x + i) % 4, core)
        else:
            ref, device = ig.at[l_], grp_of((lo + i - 3) % 4, x, core)
        return remote(ref, ref, ig_sems, (i,), device)

    def multiply(h_ref, buf, w_ref, half_of):
        def body(i, carry):
            k = ((y + i) % 4) * 2 + half_of
            piece = w_ref[pl.ds(4 * k, 4)].reshape(512, COLS)
            h_ref[...] += jnp.dot(buf[k], piece, preferred_element_type=F32)
            return carry

        lax.fori_loop(0, 4, body, 0)

    def turn(half_of):
        def body(i, carry):
            k = ((y + i) % 4) * 2 + half_of
            turned = a_e[k].T
            for b in range(4):
                at = (half_of * 2 + b // 2) * 8 + (b % 2) * 4 + (y + i) % 4
                a_t[at] = turned[b * 128 : b * 128 + 128, :]
            return carry

        lax.fori_loop(0, 4, body, 0)

    def y_pass(k):
        for i in (0, 2):
            y_arrival(k, i).wait_recv()
            y_copy(k, 4 + i // 2).start()

    def y_rest(k):
        for i in (1, 3, 4, 5):
            y_arrival(k, i).wait_recv()

    for i in (0, 1):
        locals_[i].wait()
    wz_first(0)
    for i in (0, 2, 1, 3):
        y_copy(0, i).start()
    for half in (0, 1):
        far_copy(0, half, t).start()
    w_spread(0, 0)
    for i in (2, 3, 4):
        locals_[i].wait()
    for i in (0, 2, 1, 3):
        y_copy(1, i).start()
    w_spread(1, 0)
    wz_step(0, 0)
    for i in (5, 6, 7):
        locals_[i].wait()
    h_s[...] = r_s[...].astype(F32)
    h_e[...] = r_e[...].astype(F32)
    wz_step(0, 1)
    y_pass(0)
    wz_step(0, 2)
    y_pass(1)
    w_pass(0, 0)
    far_copy(0, 0, t_far).wait_recv()
    for i in (0, 3):
        y_copy(2, i).start()
    far_copy(1, 0, t).start()
    wz_first(1)
    for b in (1, 4):
        w_pass(0, b)
    far_copy(0, 1, t_far).wait_recv()
    for i in (2, 1):
        y_copy(2, i).start()
    far_copy(1, 1, t).start()
    wz_step(1, 0)
    for b in (2, 5, 3, 6):
        w_pass(0, b)
    w_pass(1, 0)
    wz_step(1, 1)
    y_pass(2)
    w_done(0)
    wz_step(1, 2)
    y_rest(0)
    multiply(h_s, a_s, w_s, hi)
    for b in (1, 4):
        w_pass(1, b)
    y_rest(1)
    far_copy(1, 0, t_far).wait_recv()
    for i in (0, 3):
        y_copy(3, i).start()
    far_copy(1, 1, t_far).wait_recv()
    for i in (2, 1):
        y_copy(3, i).start()
    for b in (2, 5, 3, 6):
        w_pass(1, b)
    y_rest(2)
    multiply(h_s, a_s, w_s, 1 - hi)

    ar_s[t] = jnp.zeros((8, 128), F32)
    for b in range(4):
        ar_s[t, b : b + 1, :] = square_rows(h_s, b)
    ar_start(0, ar_s)
    y_pass(3)
    turn(hi)
    gain = gain_ref[...].astype(F32)

    factor_s = lax.rsqrt(ar_finish(0, ar_s) / WIDTH + EPS)
    ar_p[t] = jnp.zeros((8, 128), F32)
    for s in range(2):
        count = pass_len[s]
        total = jnp.zeros((1, COLS), F32)
        for b in range(2):
            rows = lax.broadcasted_iota(jnp.int32, (128, 128), 0) + b * 128
            col = spread_rows(factor_s[2 * s + b : 2 * s + b + 1, :])
            col = jnp.where(rows < count, col, 0.0)
            part = h_s[pl.ds((2 * s + b) * 128, 128), :] * lanes4(col)
            total = total + jnp.sum(part, axis=0, keepdims=True)
        total = total * gain / jnp.full((1, COLS), count, jnp.int32).astype(F32)
        pool_s[s : s + 1, :] = total
        square = jnp.sum(total * total, axis=1, keepdims=True)
        ar_p[t, s : s + 1, :] = jnp.broadcast_to(square, (1, 128))
    ar_start(1, ar_p)
    w_done(1)
    multiply(h_e, a_e, w_o, hi)
    norm_s = lax.rsqrt(ar_finish(1, ar_p) / WIDTH + EPS)
    for s in range(2):
        row = (pool_s[s : s + 1, :] * lanes4(norm_s[s : s + 1, :])).astype(BF16).astype(F32)
        pool_s[s : s + 1, :] = row
        for b in range(4):
            ig[lo, x * 2 + core, 4 * s + b : 4 * s + b + 1, :] = row[:, b * 128 : b * 128 + 128]
    index_ref[...] = pool_s[0:2, :].astype(BF16)
    ig_copy(0, lo, x, core).start()
    ig_copy(0, lo, x, 1 - core).wait_recv()
    for i in (2, 1, 3):
        ig_copy(i, lo, x, core).start()

    y_rest(3)
    multiply(h_e, a_e, w_o, 1 - hi)
    ar_e[t] = jnp.zeros((8, 128), F32)
    for b in range(3):
        ar_e[t, b : b + 1, :] = square_rows(h_e, b)
    ar_start(2, ar_e)
    for i in (1, 2, 3):
        ig_copy(i, lo, (x - i + 4) % 4, core).wait_recv()
    for i in (5, 4, 6):
        ig_copy(i, lo, x, core).start()
    turn(1 - hi)

    factor = lax.rsqrt(ar_finish(2, ar_e) / WIDTH + EPS)
    f_row[...] = factor
    for b in range(3):
        fcol[pl.ds(b * 128, 128), :] = spread_rows(factor[b : b + 1, :])
    for r, (first, count) in enumerate(((0, 64), (64, 64), (128, 128), (256, 128))):
        part = h_e[pl.ds(first, count), :] * lanes4(fcol[pl.ds(first, count), :])
        vec[r : r + 1, :] = jnp.sum(part, axis=0, keepdims=True) * gain / count
    for i in (4, 5, 6):
        ig_copy(i, (lo - i + 3 + 4) % 4, x, core).wait_recv()
    for r in range(2):
        for j in range(8):
            name = neg_ids[r, j]
            owner = block_owner[name // 2]
            tile = ig[owner // 8, owner % 8]
            piece = jnp.where(name % 2 == 0, tile[0:4, :], tile[4:8, :])
            at = 8 + 8 * r + j
            for b in range(4):
                vec[at : at + 1, b * 128 : b * 128 + 128] = piece[b : b + 1, :]

    nt = (((1,), (1,)), ((), ()))
    vec_g[...] = vec[0:32, :] * gain
    sims = lax.dot_general(vec_g[...], h_e[...], nt, precision=HI, preferred_element_type=F32)
    gram = lax.dot_general(vec[0:8, :], vec[...], nt, precision=HI, preferred_element_type=F32)
    first = lax.broadcasted_iota(jnp.int32, (1, 128), 1) < 64
    ar_g[t, 0:8, :] = jnp.where(first, sims[8:16, 0:128], sims[16:24, 0:128])
    ar_g[t, 8:16, :] = jnp.zeros((8, 128), F32)
    ar_g[t, 8:9, :] = jnp.where(first, sims[0:1, 0:128], sims[1:2, 0:128])
    ar_g[t, 9:10, :] = jnp.where(first, sims[2:3, 0:128], sims[3:4, 0:128])
    ar_g[t, 10:11, :] = sims[0:1, 128:256]
    ar_g[t, 11:12, :] = sims[2:3, 128:256]
    ar_g[t, 12:13, :] = sims[1:2, 256:384]
    ar_g[t, 13:14, :] = sims[3:4, 256:384]
    ar_g[t, 16:24, :] = gram
    ar_start(3, ar_g)
    both = ar_finish(3, ar_g)

    gram = both[16:24, :]
    row = lax.broadcasted_iota(jnp.int32, (8, 128), 0)
    lane = lax.broadcasted_iota(jnp.int32, (8, 128), 1)
    diag = jnp.where((lane == row) & (row < 4), gram, 0.0)
    norm_row = lax.rsqrt(jnp.sum(diag, axis=1, keepdims=True) / WIDTH + EPS)
    norm_lane = lax.rsqrt(jnp.sum(diag, axis=0, keepdims=True) / WIDTH + EPS)
    norm_lane = jnp.where(lane < 4, norm_lane, 1.0)
    unit = gram * norm_row * norm_lane
    is_pos = (lane == row + 2) & (row < 2)
    is_neg = (lane >= 8 + 8 * row) & (lane < 16 + 8 * row) & (row < 2)
    pos = jnp.sum(jnp.where(is_pos, unit, 0.0), axis=1, keepdims=True) * SCALE
    exp_neg = jnp.where(is_neg, jnp.exp(jnp.where(is_neg, unit, 0.0) * SCALE), 0.0)
    exp_pos = jnp.exp(pos)
    total = exp_pos + jnp.sum(exp_neg, axis=1, keepdims=True)
    terms = jnp.where(row < 2, jnp.log(total) - pos, 0.0)
    loss = jnp.sum(terms, axis=0, keepdims=True)
    d_pos = jnp.where(is_pos, exp_pos / total - 1.0, 0.0)
    pos_lane = jnp.sum(d_pos, axis=0, keepdims=True)
    pos_row = jnp.sum(jnp.where(lane == row, pos_lane, 0.0), axis=1, keepdims=True)
    coef = d_pos + exp_neg / total
    coef = coef + jnp.where((lane == row - 2) & (row < 4), pos_row, 0.0)
    coef = coef * SCALE
    back = jnp.sum(coef * unit, axis=1, keepdims=True) / WIDTH
    coef = norm_row * (coef * norm_lane - jnp.where(lane == row, back * norm_row, 0.0))
    coef = jnp.where(row < 4, coef, 0.0)
    coef = coef / jnp.where(row < 2, 64.0, 128.0)

    l_c[core] = jnp.broadcast_to(loss, (8, 128))
    pair_loss = remote(
        l_c.at[core], l_c.at[core], ls_sems, (0,), grp_of(lo, x, 1 - core)
    )
    pair_loss.start()

    s_full[8:16, 0:128] = both[0:8, :]
    s_full[16:24, 0:128] = both[0:8, :]
    s_full[0:2, 0:128] = jnp.broadcast_to(both[8:9, :], (2, 128))
    s_full[2:4, 0:128] = jnp.broadcast_to(both[9:10, :], (2, 128))
    s_full[0:1, 128:256] = both[10:11, :]
    s_full[2:3, 128:256] = both[11:12, :]
    s_full[1:2, 256:384] = both[12:13, :]
    s_full[3:4, 256:384] = both[13:14, :]
    inner = jnp.dot(coef, s_full[...], precision=HI, preferred_element_type=F32)
    urow[...] = jnp.dot(coef, vec[...], precision=HI, preferred_element_type=F32) * gain
    wanted = (
        ((row == 0) & (lane < 64)) | ((row == 1) & (lane >= 64)),
        row == 2,
        row == 3,
    )
    for b in range(3):
        line = jnp.sum(
            jnp.where(wanted[b], inner[:, b * 128 : b * 128 + 128], 0.0), axis=0, keepdims=True
        )
        f = f_row[b : b + 1, :]
        gcol[pl.ds(b * 128, 128), :] = spread_rows(line * f * f / WIDTH)
    for r, (first, count) in enumerate(((0, 64), (64, 64), (128, 128), (256, 128))):
        at = pl.ds(first, count)
        part = urow[r : r + 1, :] - h_e[at, :] * lanes4(gcol[at, :])
        dh[at, :] = (lanes4(fcol[at, :]) * part).astype(BF16)

    def pc_copy(i, x_):
        return remote(
            psend.at[x_], precv.at[x_], pc_sems, (i,), grp_of(lo, x, 1 - core)
        )

    up = {2: 1, 1: 1, 3: -1, 0: -1}

    def px_copy(stage, side, d):
        at = stage + side
        return remote(
            xsend.at[at, d], xrecv.at[at, d], px_sems, (at, d),
            grp_of(lo, (x + (up[d], 1, -1)[at] + 4) % 4, core),
        )

    def pz_copy(d):
        return remote(
            zsend.at[d], zrecv.at[d], pz_sems, (d,), grp_of((lo + d) % 4, x, core)
        )

    turns = (2, 1, 3, 0)
    for i in range(4):
        x_ = (x + turns[i]) % 4
        at = pl.ds((x_ * 2 + 1 - core) * 4, 4)
        part = jnp.dot(a_t[at].reshape(512, ETOK), dh[...], preferred_element_type=F32)
        psend[x_] = part.astype(BF16).reshape(4, 128, COLS)
        pc_copy(i, x_).start()
        at = pl.ds((x_ * 2 + core) * 4, 4)
        part = jnp.dot(a_t[at].reshape(512, ETOK), dh[...], preferred_element_type=F32)
        own[x_] = part.reshape(4, 128, COLS)

    pair_loss.wait_recv()
    l_x[x] = l_c[0] + l_c[1]

    def lx_copy(d, slot):
        return remote(
            l_x.at[slot], l_x.at[slot], ls_sems, (d,), grp_of(lo, (x + d) % 4, core)
        )

    def lz_copy(d, slot):
        return remote(
            l_z.at[slot], l_z.at[slot], ls_sems, (3 + d,),
            grp_of((lo + d) % 4, x, core),
        )

    for d in (1, 2, 3):
        lx_copy(d, x).start()
    def pair_sum(x_, d):
        l_ = (lo + d) % 4
        return own[x_, l_] + precv[x_, l_].astype(F32)

    pc_copy(0, x).wait_recv()
    for d in (2, 3, 1, 0):
        xsend[0, d] = pair_sum((x + 2) % 4, d).astype(BF16)
        px_copy(0, 0, d).start()
    pc_copy(1, x).wait_recv()
    for d in (3, 0):
        xsend[1, d] = pair_sum((x + 1) % 4, d).astype(BF16)
        px_copy(1, 0, d).start()
    pc_copy(2, x).wait_recv()
    for d in (2, 1):
        xsend[2, d] = pair_sum((x + 3) % 4, d).astype(BF16)
        px_copy(1, 1, d).start()
    for d in (1, 2, 3):
        lx_copy(d, (x - d + 4) % 4).wait_recv()
    l_z[lo] = (l_x[0] + l_x[1]) + (l_x[2] + l_x[3])
    for d in (1, 2, 3):
        lz_copy(d, lo).start()
    for d in (2, 3, 1, 0):
        side = 0 if up[d] == 1 else 1
        px_copy(0, 0, d).wait_recv()
        total = pair_sum((x + up[d] + 4) % 4, d) + xrecv[0, d].astype(F32)
        xsend[1 + side, d] = total.astype(BF16)
        px_copy(1, side, d).start()
    pc_copy(3, x).wait_recv()
    for d in (2, 3, 1, 0):
        total = pair_sum(x, d)
        for side in (0, 1):
            px_copy(1, side, d).wait_recv()
        total = total + (xrecv[1, d].astype(F32) + xrecv[2, d].astype(F32))
        if d == 0:
            grad_ref[...] = total
        else:
            zsend[d] = total.astype(BF16)
            pz_copy(d).start()
    for d in (1, 2, 3):
        lz_copy(d, (lo - d + 4) % 4).wait_recv()
    loss_ref[...] = ((l_z[0] + l_z[1]) + (l_z[2] + l_z[3]))[0:1, 0:1] / 64.0
    for d in (1, 3, 2):
        pz_copy(d).wait_recv()
    grad_ref[...] += (zrecv[1].astype(F32) + zrecv[2].astype(F32)) + zrecv[3].astype(F32)

    for copy in sent:
        copy.wait_send()


def shards(
    q_attn, q_resid, p_attn, p_resid, w_out, w_snap, norm_gain, pass_attn, pass_resid,
    pass_len, block_owner, neg_ids,
):
    hbm = pl.BlockSpec(memory_space=pl.ANY)
    vmem = pl.BlockSpec(memory_space=pltpu.VMEM)
    smem = pl.BlockSpec(memory_space=pltpu.SMEM)
    dma = pltpu.SemaphoreType.DMA

    def both(shape):
        return (dma(shape), dma(shape))

    loss, grad, index = pl.pallas_call(
        kernel,
        out_shape=(
            jax.ShapeDtypeStruct((1, 1), F32),
            jax.ShapeDtypeStruct((128, COLS), F32),
            jax.ShapeDtypeStruct((2, COLS), BF16),
        ),
        in_specs=[hbm] * 6 + [vmem] + [hbm] * 2 + [smem] * 3,
        out_specs=(vmem, vmem, vmem),
        scratch_shapes=[
            pltpu.VMEM((8, STOK, COLS), BF16),
            pltpu.VMEM((8, ETOK, COLS), BF16),
            pltpu.VMEM((32, 128, COLS), BF16),
            pltpu.VMEM((32, 128, COLS), BF16),
            pltpu.VMEM((STOK, COLS), BF16),
            pltpu.VMEM((ETOK, COLS), BF16),
            pltpu.VMEM((STOK, COLS), F32),
            pltpu.VMEM((ETOK, COLS), F32),
            pltpu.VMEM((32, 128, ETOK), BF16),
            pltpu.VMEM((8, 8, 128), F32),
            pltpu.VMEM((8, 8, 128), F32),
            pltpu.VMEM((8, 8, 128), F32),
            pltpu.VMEM((8, 24, 128), F32),
            pltpu.VMEM((4, 8, 8, 128), F32),
            pltpu.VMEM((8, COLS), F32),
            pltpu.VMEM((128, COLS), F32),
            pltpu.VMEM((32, COLS), F32),
            pltpu.VMEM((128, ETOK), F32),
            pltpu.VMEM((ETOK, 128), F32),
            pltpu.VMEM((ETOK, 128), F32),
            pltpu.VMEM((8, 128), F32),
            pltpu.VMEM((8, COLS), F32),
            pltpu.VMEM((ETOK, COLS), BF16),
            pltpu.VMEM((4, 4, 128, COLS), F32),
            pltpu.VMEM((4, 4, 128, COLS), BF16),
            pltpu.VMEM((4, 4, 128, COLS), BF16),
            pltpu.VMEM((3, 4, 128, COLS), BF16),
            pltpu.VMEM((3, 4, 128, COLS), BF16),
            pltpu.VMEM((4, 128, COLS), BF16),
            pltpu.VMEM((4, 128, COLS), BF16),
            pltpu.VMEM((2, 8, 128), F32),
            pltpu.VMEM((4, 8, 128), F32),
            pltpu.VMEM((4, 8, 128), F32),
            dma((8,)),
            both((4, 6)),
            both((2, 2)),
            both((2, 2, 3)),
            both((2, 7, 4)),
            both((2, 7, 4)),
            both((4, 8)),
            both((7,)),
            both((4,)),
            both((3, 4)),
            both((4,)),
            both((7,)),
        ],
        compiler_params=pltpu.CompilerParams(
            collective_id=0, has_side_effects=True, vmem_limit_bytes=56 * 2**20
        ),
    )(
        q_attn.reshape(128, COLS),
        q_resid.reshape(128, COLS),
        p_attn.reshape(256, COLS),
        p_resid.reshape(256, COLS),
        w_out,
        w_snap,
        norm_gain.reshape(1, COLS),
        pass_attn.reshape(STOK, COLS),
        pass_resid.reshape(STOK, COLS),
        pass_len,
        block_owner,
        neg_ids,
    )
    return (loss[0, 0], grad, index)


def solution(mesh):
    placed = (
        P("grp", None, "tp"),
        P("grp", None, "tp"),
        P("grp", None, "tp"),
        P("grp", None, "tp"),
        P("grp", "tp"),
        P("grp", "tp"),
        P("tp"),
        P("grp", None, "tp"),
        P("grp", None, "tp"),
        P("grp"),
        P(),
        P("grp", None),
    )
    return jax.shard_map(
        shards,
        mesh=mesh,
        in_specs=placed,
        out_specs=(P(), P("grp", "tp"), P("grp", "tp")),
        check_vma=False,
    )
```

```python
import functools

import jax
import jax.numpy as jnp
from jax import lax
from jax.experimental import pallas as pl
from jax.experimental.pallas import tpu as pltpu
from jax.sharding import PartitionSpec as P

EPS = 1e-06
TEMP = 0.05
WIDTH = 4096
COLS = 512
STOK = 512
ETOK = 384
SCALE = 1.0 / (WIDTH * TEMP)
MESH = pl.DeviceIdType.MESH
HI = lax.Precision.HIGHEST
F32 = jnp.float32
BF16 = jnp.bfloat16
PARTS = 7


class Copy:
    def __init__(self, sent, src, dst, sems, at, device):
        self.sent = sent
        self.key = (id(sems), at)
        self.copy = pltpu.make_async_remote_copy(
            src_ref=src, dst_ref=dst, send_sem=sems[0].at[at], recv_sem=sems[1].at[at],
            device_id=device, device_id_type=MESH,
        )

    def start(self, when=None):
        self.when = when
        self.sent.append(self)
        self.guard(when, self.copy.start)

    def wait_recv(self, when=None):
        self.guard(when, self.copy.wait_recv)

    def wait_send(self):
        self.guard(self.when, self.copy.wait_send)

    def guard(self, when, action):
        if when is None:
            action()
        else:
            pl.when(when)(action)


def lanes4(col):
    return jnp.concatenate([col, col, col, col], axis=1)


def spread_rows(row):
    return jnp.broadcast_to(row, (128, 128)).T


def square_rows(h_ref, block):
    part = h_ref[pl.ds(block * 128, 128), :]
    part = part * part
    part = (part[:, 0:128] + part[:, 128:256]) + (part[:, 256:384] + part[:, 384:512])
    return jnp.sum(part.T, axis=0, keepdims=True)


def kernel(
    q_attn, q_resid, p_attn, p_resid, w_out, w_snap, gain_ref, s_attn, s_resid,
    pass_len, block_owner, neg_ids,
    loss_ref, grad_ref, index_ref,
    a_s, a_e, w_s, w_o, r_s, r_e, h_s, h_e, a_t,
    ar_s, ar_p, ar_e, ar_g, ig, pool_s, vec, vec_g, s_full, fcol, gcol, f_row, urow, dh,
    own, psend, precv, xsend, xrecv, zsend, zrecv, l_c, l_x, l_z,
    loc, y_sems, z_sems, wz_sems, wx_sems, wc_sems, ar_sems, ig_sems, pc_sems, px_sems, pz_sems,
    ls_sems,
):
    grp = lax.axis_index("grp")
    t = lax.axis_index("tp")
    core = grp % 2
    x = (grp // 2) % 4
    lo = grp // 8
    y = t // 2
    hi = t % 2
    t_far = y * 2 + (1 - hi)

    def grp_of(l_, x_, c_):
        return (l_ * 8 + x_ * 2 + c_, t)

    def tp_of(y_, h_):
        return (grp, y_ * 2 + h_)

    sent = []

    def remote(src, dst, sems, at, device):
        return Copy(sent, src, dst, sems, at, device)

    locals_ = [
        pltpu.make_async_copy(w_snap, w_s.at[grp], loc.at[0]),
        pltpu.make_async_copy(s_attn, a_s.at[t], loc.at[1]),
        pltpu.make_async_copy(w_out, w_o.at[grp], loc.at[2]),
        pltpu.make_async_copy(q_attn, a_e.at[t, pl.ds(0, 128)], loc.at[3]),
        pltpu.make_async_copy(p_attn, a_e.at[t, pl.ds(128, 256)], loc.at[4]),
        pltpu.make_async_copy(s_resid, r_s, loc.at[5]),
        pltpu.make_async_copy(q_resid, r_e.at[pl.ds(0, 128)], loc.at[6]),
        pltpu.make_async_copy(p_resid, r_e.at[pl.ds(128, 256)], loc.at[7]),
    ]
    for copy in locals_:
        copy.start()

    barrier = pltpu.get_barrier_semaphore()
    peers = [grp_of(lo, x, 1 - core)]
    for d in (1, 2, 3):
        peers.append(grp_of(lo, (x + d) % 4, core))
        peers.append(grp_of((lo + d) % 4, x, core))
        peers.append(tp_of((y + d) % 4, hi))
    peers.append(tp_of(y, 1 - hi))
    for peer in peers:
        pl.semaphore_signal(barrier, inc=1, device_id=peer, device_id_type=MESH)
    vec[...] = jnp.zeros_like(vec)
    s_full[...] = jnp.zeros_like(s_full)
    pl.semaphore_wait(barrier, len(peers))

    def token_part(part, slot):
        if part < 4:
            return a_s.at[slot, pl.ds(part * 128, 128)]
        return a_e.at[slot, pl.ds((part - 4) * 128, 128)]

    def pass_step(far, part):
        return 1 if (part + far) % 2 == 0 else -1

    def y_copy(far, part, way):
        step = (1, -1, pass_step(far, part))[way]
        row = y if way < 2 else (y - step + 4) % 4
        ref = token_part(part, row * 2 + (hi if far == 0 else 1 - hi))
        return remote(ref, ref, y_sems, (far, part, way), tp_of((y + step + 4) % 4, hi))

    def y_arrival(far, part, way):
        step = (1, -1, 2 * pass_step(far, part))[way]
        ref = token_part(part, ((y - step + 4) % 4) * 2 + (hi if far == 0 else 1 - hi))
        return remote(ref, ref, y_sems, (far, part, way), tp_of(y, hi))

    def y_send(far, part):
        first = 0 if pass_step(far, part) == 1 else 1
        y_copy(far, part, first).start()
        y_copy(far, part, 1 - first).start()

    def y_pass(far, part):
        way = 0 if pass_step(far, part) == 1 else 1
        y_arrival(far, part, way).wait_recv()
        y_copy(far, part, 2).start()

    def y_rest(far, parts):
        for part in parts:
            y_arrival(far, part, 1 if pass_step(far, part) == 1 else 0).wait_recv()
            y_arrival(far, part, 2).wait_recv()

    def far_copy(part, slot):
        ref = token_part(part, slot)
        return remote(ref, ref, z_sems, (part,), tp_of(y, 1 - hi))

    def far_pass(part):
        far_copy(part, t_far).wait_recv()
        if part + 3 < PARTS:
            far_copy(part + 3, t).start()
        y_send(1, part)

    weights = (w_s, w_o)

    def wz_copy(m, way, step, source):
        ref = weights[m].at[source * 8 + x * 2 + core]
        return remote(
            ref, ref, wz_sems, (m, way, step),
            grp_of((lo + (1, 3)[way]) % 4, x, core),
        )

    def wz_first(m):
        wz_copy(m, 0, 0, lo).start(lo < 3)
        wz_copy(m, 1, 0, lo).start(lo > 0)

    def wz_step(m, step):
        for way in (0, 1):
            source = (lo + (step + 1) * (-1, 1)[way] + 4) % 4
            came = (lo > step, lo < 3 - step)[way]
            wz_copy(m, way, step, source).wait_recv(came)
            if step < 2:
                wz_copy(m, way, step + 1, source).start(came & (lo < 3, lo > 0)[way])
            for d in (2, 1, 3):
                wx_copy(m, 1 + 3 * way + step, d, x).start(came)
            wc_copy(m, 1 + 3 * way + step, 0, core).start(came)

    def line(b):
        if b == 0:
            return lo, None
        step = (b - 1) % 3
        way = (b - 1) // 3
        return (lo + (step + 1) * (-1, 1)[way] + 4) % 4, (lo > step, lo < 3 - step)[way]

    def w_pass(m, b):
        for d in (1, 3, 2):
            wx_copy(m, b, d, (x - d + 4) % 4).wait_recv(line(b)[1])
            wc_copy(m, b, d, core).start(line(b)[1])

    def w_done(m):
        for b in range(7):
            for d in range(4):
                wc_copy(m, b, d, 1 - core).wait_recv(line(b)[1])

    def wx_copy(m, b, d, x_):
        ref = weights[m].at[line(b)[0] * 8 + x_ * 2 + core]
        return remote(
            ref, ref, wx_sems, (m, b, d), grp_of(lo, (x + d) % 4, core)
        )

    def wc_copy(m, b, d, c_):
        ref = weights[m].at[line(b)[0] * 8 + ((x - d + 4) % 4) * 2 + c_]
        return remote(
            ref, ref, wc_sems, (m, b, d), grp_of(lo, x, 1 - core)
        )

    def w_spread(m, b):
        for d in (2, 1, 3):
            wx_copy(m, b, d, x).start()
        wc_copy(m, b, 0, core).start()

    def ar_copy(which, buf, j, slot):
        ref = buf.at[slot]
        return remote(
            ref, ref, ar_sems, (which, j),
            tp_of((y + j // 2) % 4, (hi + j % 2) % 2),
        )

    def ar_start(which, buf):
        for j in (5, 7, 3, 4, 1, 2, 6):
            ar_copy(which, buf, j, t).start()

    def ar_finish(which, buf):
        for j in range(1, 8):
            ar_copy(which, buf, j, ((y - j // 2 + 4) % 4) * 2 + (hi + j % 2) % 2).wait_recv()
        total = buf[0]
        for j in range(1, 8):
            total = total + buf[j]
        return total

    def ig_copy(i, l_, x_, c_):
        if i == 0:
            ref, device = ig.at[lo, x * 2 + c_], grp_of(lo, x, 1 - core)
        elif i < 4:
            ref, device = ig.at[lo, pl.ds(x_ * 2, 2)], grp_of(lo, (x + i) % 4, core)
        else:
            ref, device = ig.at[l_], grp_of((lo + i - 3) % 4, x, core)
        return remote(ref, ref, ig_sems, (i,), device)

    def multiply(h_ref, buf, w_ref, half_of):
        def body(i, carry):
            k = ((y + i) % 4) * 2 + half_of
            piece = w_ref[pl.ds(4 * k, 4)].reshape(512, COLS)
            h_ref[...] += jnp.dot(buf[k], piece, preferred_element_type=F32)
            return carry

        lax.fori_loop(0, 4, body, 0)

    def turn(half_of):
        def body(i, carry):
            k = ((y + i) % 4) * 2 + half_of
            turned = a_e[k].T
            for b in range(4):
                at = (half_of * 2 + b // 2) * 8 + (b % 2) * 4 + (y + i) % 4
                a_t[at] = turned[b * 128 : b * 128 + 128, :]
            return carry

        lax.fori_loop(0, 4, body, 0)

    for i in (0, 1):
        locals_[i].wait()
    wz_first(0)
    for part in range(4):
        y_send(0, part)
        if part < 3:
            far_copy(part, t).start()
    w_spread(0, 0)
    for i in (2, 3, 4):
        locals_[i].wait()
    for part in (4, 5, 6):
        y_send(0, part)
    w_spread(1, 0)
    wz_step(0, 0)
    for i in (5, 6, 7):
        locals_[i].wait()
    h_s[...] = r_s[...].astype(F32)
    h_e[...] = r_e[...].astype(F32)
    y_pass(0, 0)
    y_pass(0, 1)
    wz_step(0, 1)
    far_pass(0)
    y_pass(0, 2)
    y_pass(0, 3)
    far_pass(1)
    wz_step(0, 2)
    wz_first(1)
    for b in (0, 1, 4):
        w_pass(0, b)
    far_pass(2)
    for part in (4, 5, 6):
        y_pass(0, part)
    for b in (2, 5):
        w_pass(0, b)
    far_pass(3)
    for b in (3, 6):
        w_pass(0, b)
    w_pass(1, 0)
    y_pass(1, 0)
    y_pass(1, 1)
    far_pass(4)
    wz_step(1, 0)
    w_done(0)
    y_rest(0, range(4))
    multiply(h_s, a_s, w_s, hi)
    y_pass(1, 2)
    y_pass(1, 3)
    far_pass(5)
    wz_step(1, 1)
    for b in (1, 4):
        w_pass(1, b)
    y_rest(1, range(4))
    multiply(h_s, a_s, w_s, 1 - hi)

    ar_s[t] = jnp.zeros((8, 128), F32)
    for b in range(4):
        ar_s[t, b : b + 1, :] = square_rows(h_s, b)
    ar_start(0, ar_s)
    y_pass(1, 4)
    far_pass(6)
    wz_step(1, 2)
    y_pass(1, 5)
    y_rest(0, (4, 5, 6))
    turn(hi)
    for b in (2, 5):
        w_pass(1, b)
    gain = gain_ref[...].astype(F32)

    factor_s = lax.rsqrt(ar_finish(0, ar_s) / WIDTH + EPS)
    ar_p[t] = jnp.zeros((8, 128), F32)
    for s in range(2):
        count = pass_len[s]
        total = jnp.zeros((1, COLS), F32)
        for b in range(2):
            rows = lax.broadcasted_iota(jnp.int32, (128, 128), 0) + b * 128
            col = spread_rows(factor_s[2 * s + b : 2 * s + b + 1, :])
            col = jnp.where(rows < count, col, 0.0)
            part = h_s[pl.ds((2 * s + b) * 128, 128), :] * lanes4(col)
            total = total + jnp.sum(part, axis=0, keepdims=True)
        total = total * gain / jnp.full((1, COLS), count, jnp.int32).astype(F32)
        pool_s[s : s + 1, :] = total
        square = jnp.sum(total * total, axis=1, keepdims=True)
        ar_p[t, s : s + 1, :] = jnp.broadcast_to(square, (1, 128))
    ar_start(1, ar_p)
    y_pass(1, 6)
    for b in (3, 6):
        w_pass(1, b)
    w_done(1)
    multiply(h_e, a_e, w_o, hi)
    norm_s = lax.rsqrt(ar_finish(1, ar_p) / WIDTH + EPS)
    for s in range(2):
        row = (pool_s[s : s + 1, :] * lanes4(norm_s[s : s + 1, :])).astype(BF16).astype(F32)
        pool_s[s : s + 1, :] = row
        for b in range(4):
            ig[lo, x * 2 + core, 4 * s + b : 4 * s + b + 1, :] = row[:, b * 128 : b * 128 + 128]
    index_ref[...] = pool_s[0:2, :].astype(BF16)
    ig_copy(0, lo, x, core).start()
    ig_copy(0, lo, x, 1 - core).wait_recv()
    for i in (2, 1, 3):
        ig_copy(i, lo, x, core).start()

    y_rest(1, (4, 5, 6))
    multiply(h_e, a_e, w_o, 1 - hi)
    ar_e[t] = jnp.zeros((8, 128), F32)
    for b in range(3):
        ar_e[t, b : b + 1, :] = square_rows(h_e, b)
    ar_start(2, ar_e)
    for i in (1, 2, 3):
        ig_copy(i, lo, (x - i + 4) % 4, core).wait_recv()
    for i in (5, 4, 6):
        ig_copy(i, lo, x, core).start()
    turn(1 - hi)

    factor = lax.rsqrt(ar_finish(2, ar_e) / WIDTH + EPS)
    f_row[...] = factor
    for b in range(3):
        fcol[pl.ds(b * 128, 128), :] = spread_rows(factor[b : b + 1, :])
    for r, (first, count) in enumerate(((0, 64), (64, 64), (128, 128), (256, 128))):
        part = h_e[pl.ds(first, count), :] * lanes4(fcol[pl.ds(first, count), :])
        vec[r : r + 1, :] = jnp.sum(part, axis=0, keepdims=True) * gain / count
    for i in (4, 5, 6):
        ig_copy(i, (lo - i + 3 + 4) % 4, x, core).wait_recv()
    for r in range(2):
        for j in range(8):
            name = neg_ids[r, j]
            owner = block_owner[name // 2]
            tile = ig[owner // 8, owner % 8]
            piece = jnp.where(name % 2 == 0, tile[0:4, :], tile[4:8, :])
            at = 8 + 8 * r + j
            for b in range(4):
                vec[at : at + 1, b * 128 : b * 128 + 128] = piece[b : b + 1, :]

    nt = (((1,), (1,)), ((), ()))
    vec_g[...] = vec[0:32, :] * gain
    sims = lax.dot_general(vec_g[...], h_e[...], nt, precision=HI, preferred_element_type=F32)
    gram = lax.dot_general(vec[0:8, :], vec[...], nt, precision=HI, preferred_element_type=F32)
    first = lax.broadcasted_iota(jnp.int32, (1, 128), 1) < 64
    ar_g[t, 0:8, :] = jnp.where(first, sims[8:16, 0:128], sims[16:24, 0:128])
    ar_g[t, 8:16, :] = jnp.zeros((8, 128), F32)
    ar_g[t, 8:9, :] = jnp.where(first, sims[0:1, 0:128], sims[1:2, 0:128])
    ar_g[t, 9:10, :] = jnp.where(first, sims[2:3, 0:128], sims[3:4, 0:128])
    ar_g[t, 10:11, :] = sims[0:1, 128:256]
    ar_g[t, 11:12, :] = sims[2:3, 128:256]
    ar_g[t, 12:13, :] = sims[1:2, 256:384]
    ar_g[t, 13:14, :] = sims[3:4, 256:384]
    ar_g[t, 16:24, :] = gram
    ar_start(3, ar_g)
    both = ar_finish(3, ar_g)

    gram = both[16:24, :]
    row = lax.broadcasted_iota(jnp.int32, (8, 128), 0)
    lane = lax.broadcasted_iota(jnp.int32, (8, 128), 1)
    diag = jnp.where((lane == row) & (row < 4), gram, 0.0)
    norm_row = lax.rsqrt(jnp.sum(diag, axis=1, keepdims=True) / WIDTH + EPS)
    norm_lane = lax.rsqrt(jnp.sum(diag, axis=0, keepdims=True) / WIDTH + EPS)
    norm_lane = jnp.where(lane < 4, norm_lane, 1.0)
    unit = gram * norm_row * norm_lane
    is_pos = (lane == row + 2) & (row < 2)
    is_neg = (lane >= 8 + 8 * row) & (lane < 16 + 8 * row) & (row < 2)
    pos = jnp.sum(jnp.where(is_pos, unit, 0.0), axis=1, keepdims=True) * SCALE
    exp_neg = jnp.where(is_neg, jnp.exp(jnp.where(is_neg, unit, 0.0) * SCALE), 0.0)
    exp_pos = jnp.exp(pos)
    total = exp_pos + jnp.sum(exp_neg, axis=1, keepdims=True)
    terms = jnp.where(row < 2, jnp.log(total) - pos, 0.0)
    loss = jnp.sum(terms, axis=0, keepdims=True)
    d_pos = jnp.where(is_pos, exp_pos / total - 1.0, 0.0)
    pos_lane = jnp.sum(d_pos, axis=0, keepdims=True)
    pos_row = jnp.sum(jnp.where(lane == row, pos_lane, 0.0), axis=1, keepdims=True)
    coef = d_pos + exp_neg / total
    coef = coef + jnp.where((lane == row - 2) & (row < 4), pos_row, 0.0)
    coef = coef * SCALE
    back = jnp.sum(coef * unit, axis=1, keepdims=True) / WIDTH
    coef = norm_row * (coef * norm_lane - jnp.where(lane == row, back * norm_row, 0.0))
    coef = jnp.where(row < 4, coef, 0.0)
    coef = coef / jnp.where(row < 2, 64.0, 128.0)

    l_c[core] = jnp.broadcast_to(loss, (8, 128))
    pair_loss = remote(
        l_c.at[core], l_c.at[core], ls_sems, (0,), grp_of(lo, x, 1 - core)
    )
    pair_loss.start()

    s_full[8:16, 0:128] = both[0:8, :]
    s_full[16:24, 0:128] = both[0:8, :]
    s_full[0:2, 0:128] = jnp.broadcast_to(both[8:9, :], (2, 128))
    s_full[2:4, 0:128] = jnp.broadcast_to(both[9:10, :], (2, 128))
    s_full[0:1, 128:256] = both[10:11, :]
    s_full[2:3, 128:256] = both[11:12, :]
    s_full[1:2, 256:384] = both[12:13, :]
    s_full[3:4, 256:384] = both[13:14, :]
    inner = jnp.dot(coef, s_full[...], precision=HI, preferred_element_type=F32)
    urow[...] = jnp.dot(coef, vec[...], precision=HI, preferred_element_type=F32) * gain
    wanted = (
        ((row == 0) & (lane < 64)) | ((row == 1) & (lane >= 64)),
        row == 2,
        row == 3,
    )
    for b in range(3):
        line = jnp.sum(
            jnp.where(wanted[b], inner[:, b * 128 : b * 128 + 128], 0.0), axis=0, keepdims=True
        )
        f = f_row[b : b + 1, :]
        gcol[pl.ds(b * 128, 128), :] = spread_rows(line * f * f / WIDTH)
    for r, (first, count) in enumerate(((0, 64), (64, 64), (128, 128), (256, 128))):
        at = pl.ds(first, count)
        part = urow[r : r + 1, :] - h_e[at, :] * lanes4(gcol[at, :])
        dh[at, :] = (lanes4(fcol[at, :]) * part).astype(BF16)

    def pc_copy(i, x_):
        return remote(
            psend.at[x_], precv.at[x_], pc_sems, (i,), grp_of(lo, x, 1 - core)
        )

    up = {2: 1, 1: 1, 3: -1, 0: -1}

    def px_copy(stage, side, d):
        at = stage + side
        return remote(
            xsend.at[at, d], xrecv.at[at, d], px_sems, (at, d),
            grp_of(lo, (x + (up[d], 1, -1)[at] + 4) % 4, core),
        )

    def pz_copy(d):
        return remote(
            zsend.at[d], zrecv.at[d], pz_sems, (d,), grp_of((lo + d) % 4, x, core)
        )

    turns = (2, 1, 3, 0)

    def part_of(x_, c_):
        rows = a_t[pl.ds((x_ * 2 + c_) * 4, 4)].reshape(512, ETOK)
        part = jnp.dot(rows, dh[...], preferred_element_type=F32)
        return part.reshape(4, 128, COLS)

    def give(i):
        x_ = (x + turns[i]) % 4
        psend[x_] = part_of(x_, 1 - core).astype(BF16)
        pc_copy(i, x_).start()

    def keep(i):
        x_ = (x + turns[i]) % 4
        own[x_] = part_of(x_, core)

    def pair_sum(x_, d):
        l_ = (lo + d) % 4
        return own[x_, l_] + precv[x_, l_].astype(F32)

    def direct(d):
        side = 0 if up[d] == -1 else 1
        xsend[1 + side, d] = pair_sum((x + (1, 3)[side]) % 4, d).astype(BF16)
        px_copy(1, side, d).start()

    def relay(d):
        side = 0 if up[d] == 1 else 1
        px_copy(0, 0, d).wait_recv()
        total = pair_sum((x + (1, 3)[side]) % 4, d) + xrecv[0, d].astype(F32)
        xsend[1 + side, d] = total.astype(BF16)
        px_copy(1, side, d).start()

    give(0)
    keep(0)
    give(1)
    pair_loss.wait_recv()
    l_x[x] = l_c[0] + l_c[1]

    def lx_copy(d, slot):
        return remote(
            l_x.at[slot], l_x.at[slot], ls_sems, (d,), grp_of(lo, (x + d) % 4, core)
        )

    def lz_copy(d, slot):
        return remote(
            l_z.at[slot], l_z.at[slot], ls_sems, (3 + d,),
            grp_of((lo + d) % 4, x, core),
        )

    for d in (1, 2, 3):
        lx_copy(d, x).start()
    pc_copy(0, x).wait_recv()
    for d in (2, 3, 1, 0):
        xsend[0, d] = pair_sum((x + 2) % 4, d).astype(BF16)
        px_copy(0, 0, d).start()
    keep(1)
    give(2)
    keep(2)
    give(3)
    pc_copy(1, x).wait_recv()
    pc_copy(2, x).wait_recv()
    relay(2)
    relay(3)
    direct(3)
    direct(2)
    keep(3)
    for d in (1, 2, 3):
        lx_copy(d, (x - d + 4) % 4).wait_recv()
    l_z[lo] = (l_x[0] + l_x[1]) + (l_x[2] + l_x[3])
    for d in (1, 2, 3):
        lz_copy(d, lo).start()
    relay(1)
    direct(1)
    direct(0)
    relay(0)
    pc_copy(3, x).wait_recv()
    for d in (2, 3, 1, 0):
        total = pair_sum(x, d)
        for side in (0, 1):
            px_copy(1, side, d).wait_recv()
        total = total + (xrecv[1, d].astype(F32) + xrecv[2, d].astype(F32))
        if d == 0:
            grad_ref[...] = total
        else:
            zsend[d] = total.astype(BF16)
            pz_copy(d).start()
    for d in (1, 2, 3):
        lz_copy(d, (lo - d + 4) % 4).wait_recv()
    loss_ref[...] = ((l_z[0] + l_z[1]) + (l_z[2] + l_z[3]))[0:1, 0:1] / 64.0
    for d in (1, 3, 2):
        pz_copy(d).wait_recv()
    grad_ref[...] += (zrecv[1].astype(F32) + zrecv[2].astype(F32)) + zrecv[3].astype(F32)

    for copy in sent:
        copy.wait_send()


def shards(
    q_attn, q_resid, p_attn, p_resid, w_out, w_snap, norm_gain, pass_attn, pass_resid,
    pass_len, block_owner, neg_ids,
):
    hbm = pl.BlockSpec(memory_space=pl.ANY)
    vmem = pl.BlockSpec(memory_space=pltpu.VMEM)
    smem = pl.BlockSpec(memory_space=pltpu.SMEM)
    dma = pltpu.SemaphoreType.DMA

    def both(shape):
        return (dma(shape), dma(shape))

    loss, grad, index = pl.pallas_call(
        kernel,
        out_shape=(
            jax.ShapeDtypeStruct((1, 1), F32),
            jax.ShapeDtypeStruct((128, COLS), F32),
            jax.ShapeDtypeStruct((2, COLS), BF16),
        ),
        in_specs=[hbm] * 6 + [vmem] + [hbm] * 2 + [smem] * 3,
        out_specs=(vmem, vmem, vmem),
        scratch_shapes=[
            pltpu.VMEM((8, STOK, COLS), BF16),
            pltpu.VMEM((8, ETOK, COLS), BF16),
            pltpu.VMEM((32, 128, COLS), BF16),
            pltpu.VMEM((32, 128, COLS), BF16),
            pltpu.VMEM((STOK, COLS), BF16),
            pltpu.VMEM((ETOK, COLS), BF16),
            pltpu.VMEM((STOK, COLS), F32),
            pltpu.VMEM((ETOK, COLS), F32),
            pltpu.VMEM((32, 128, ETOK), BF16),
            pltpu.VMEM((8, 8, 128), F32),
            pltpu.VMEM((8, 8, 128), F32),
            pltpu.VMEM((8, 8, 128), F32),
            pltpu.VMEM((8, 24, 128), F32),
            pltpu.VMEM((4, 8, 8, 128), F32),
            pltpu.VMEM((8, COLS), F32),
            pltpu.VMEM((128, COLS), F32),
            pltpu.VMEM((32, COLS), F32),
            pltpu.VMEM((128, ETOK), F32),
            pltpu.VMEM((ETOK, 128), F32),
            pltpu.VMEM((ETOK, 128), F32),
            pltpu.VMEM((8, 128), F32),
            pltpu.VMEM((8, COLS), F32),
            pltpu.VMEM((ETOK, COLS), BF16),
            pltpu.VMEM((4, 4, 128, COLS), F32),
            pltpu.VMEM((4, 4, 128, COLS), BF16),
            pltpu.VMEM((4, 4, 128, COLS), BF16),
            pltpu.VMEM((3, 4, 128, COLS), BF16),
            pltpu.VMEM((3, 4, 128, COLS), BF16),
            pltpu.VMEM((4, 128, COLS), BF16),
            pltpu.VMEM((4, 128, COLS), BF16),
            pltpu.VMEM((2, 8, 128), F32),
            pltpu.VMEM((4, 8, 128), F32),
            pltpu.VMEM((4, 8, 128), F32),
            dma((8,)),
            both((2, PARTS, 3)),
            both((PARTS,)),
            both((2, 2, 3)),
            both((2, 7, 4)),
            both((2, 7, 4)),
            both((4, 8)),
            both((7,)),
            both((4,)),
            both((3, 4)),
            both((4,)),
            both((7,)),
        ],
        compiler_params=pltpu.CompilerParams(
            collective_id=0, has_side_effects=True, vmem_limit_bytes=56 * 2**20
        ),
    )(
        q_attn.reshape(128, COLS),
        q_resid.reshape(128, COLS),
        p_attn.reshape(256, COLS),
        p_resid.reshape(256, COLS),
        w_out,
        w_snap,
        norm_gain.reshape(1, COLS),
        pass_attn.reshape(STOK, COLS),
        pass_resid.reshape(STOK, COLS),
        pass_len,
        block_owner,
        neg_ids,
    )
    return (loss[0, 0], grad, index)


def solution(mesh):
    placed = (
        P("grp", None, "tp"),
        P("grp", None, "tp"),
        P("grp", None, "tp"),
        P("grp", None, "tp"),
        P("grp", "tp"),
        P("grp", "tp"),
        P("tp"),
        P("grp", None, "tp"),
        P("grp", None, "tp"),
        P("grp"),
        P(),
        P("grp", None),
    )
    return jax.shard_map(
        shards,
        mesh=mesh,
        in_specs=placed,
        out_specs=(P(), P("grp", "tp"), P("grp", "tp")),
        check_vma=False,
    )
```

```python
import functools

import jax
import jax.numpy as jnp
from jax import lax
from jax.experimental import pallas as pl
from jax.experimental.pallas import tpu as pltpu
from jax.sharding import PartitionSpec as P

EPS = 1e-06
TEMP = 0.05
WIDTH = 4096
COLS = 512
STOK = 512
ETOK = 384
SCALE = 1.0 / (WIDTH * TEMP)
MESH = pl.DeviceIdType.MESH
HI = lax.Precision.HIGHEST
F32 = jnp.float32
BF16 = jnp.bfloat16
PARTS = 7


class Copy:
    def __init__(self, sent, src, dst, sems, at, device):
        self.sent = sent
        self.key = (id(sems), at)
        self.copy = pltpu.make_async_remote_copy(
            src_ref=src, dst_ref=dst, send_sem=sems[0].at[at], recv_sem=sems[1].at[at],
            device_id=device, device_id_type=MESH,
        )

    def start(self, when=None):
        self.when = when
        self.sent.append(self)
        self.guard(when, self.copy.start)

    def wait_recv(self, when=None):
        self.guard(when, self.copy.wait_recv)

    def wait_send(self):
        self.guard(self.when, self.copy.wait_send)

    def guard(self, when, action):
        if when is None:
            action()
        else:
            pl.when(when)(action)


def lanes4(col):
    return jnp.concatenate([col, col, col, col], axis=1)


def spread_rows(row):
    return jnp.broadcast_to(row, (128, 128)).T


def square_rows(h_ref, block):
    part = h_ref[pl.ds(block * 128, 128), :]
    part = part * part
    part = (part[:, 0:128] + part[:, 128:256]) + (part[:, 256:384] + part[:, 384:512])
    return jnp.sum(part.T, axis=0, keepdims=True)


def kernel(
    q_attn, q_resid, p_attn, p_resid, w_out, w_snap, gain_ref, s_attn, s_resid,
    pass_len, block_owner, neg_ids,
    loss_ref, grad_ref, index_ref,
    a_s, a_e, w_s, w_o, r_s, r_e, h_s, h_e, a_t,
    ar_s, ar_p, ar_e, ar_g, ig, pool_s, vec, vec_g, s_full, fcol, gcol, f_row, urow, dh,
    own, psend, precv, xsend, xrecv, zsend, zrecv, l_c, l_x, l_z,
    loc, y_sems, z_sems, wz_sems, wx_sems, wc_sems, ar_sems, ig_sems, pc_sems, px_sems, pz_sems,
    ls_sems,
):
    grp = lax.axis_index("grp")
    t = lax.axis_index("tp")
    core = grp % 2
    x = (grp // 2) % 4
    lo = grp // 8
    y = t // 2
    hi = t % 2
    t_far = y * 2 + (1 - hi)

    def grp_of(l_, x_, c_):
        return (l_ * 8 + x_ * 2 + c_, t)

    def tp_of(y_, h_):
        return (grp, y_ * 2 + h_)

    sent = []

    def remote(src, dst, sems, at, device):
        return Copy(sent, src, dst, sems, at, device)

    locals_ = [
        pltpu.make_async_copy(w_snap, w_s.at[grp], loc.at[0]),
        pltpu.make_async_copy(s_attn, a_s.at[t], loc.at[1]),
        pltpu.make_async_copy(w_out, w_o.at[grp], loc.at[2]),
        pltpu.make_async_copy(q_attn, a_e.at[t, pl.ds(0, 128)], loc.at[3]),
        pltpu.make_async_copy(p_attn, a_e.at[t, pl.ds(128, 256)], loc.at[4]),
        pltpu.make_async_copy(s_resid, r_s, loc.at[5]),
        pltpu.make_async_copy(q_resid, r_e.at[pl.ds(0, 128)], loc.at[6]),
        pltpu.make_async_copy(p_resid, r_e.at[pl.ds(128, 256)], loc.at[7]),
    ]
    for copy in locals_:
        copy.start()

    barrier = pltpu.get_barrier_semaphore()
    peers = [grp_of(lo, x, 1 - core)]
    for d in (1, 2, 3):
        peers.append(grp_of(lo, (x + d) % 4, core))
        peers.append(grp_of((lo + d) % 4, x, core))
        peers.append(tp_of((y + d) % 4, hi))
    peers.append(tp_of(y, 1 - hi))
    for peer in peers:
        pl.semaphore_signal(barrier, inc=1, device_id=peer, device_id_type=MESH)
    vec[...] = jnp.zeros_like(vec)
    s_full[...] = jnp.zeros_like(s_full)
    pl.semaphore_wait(barrier, len(peers))

    def token_part(part, slot):
        if part < 4:
            return a_s.at[slot, pl.ds(part * 128, 128)]
        return a_e.at[slot, pl.ds((part - 4) * 128, 128)]

    def pass_step(far, part):
        return 1 if (part + far) % 2 == 0 else -1

    def y_copy(far, part, way):
        step = (1, -1, pass_step(far, part))[way]
        row = y if way < 2 else (y - step + 4) % 4
        ref = token_part(part, row * 2 + (hi if far == 0 else 1 - hi))
        return remote(ref, ref, y_sems, (far, part, way), tp_of((y + step + 4) % 4, hi))

    def y_arrival(far, part, way):
        step = (1, -1, 2 * pass_step(far, part))[way]
        ref = token_part(part, ((y - step + 4) % 4) * 2 + (hi if far == 0 else 1 - hi))
        return remote(ref, ref, y_sems, (far, part, way), tp_of(y, hi))

    def y_send(far, part):
        first = 0 if pass_step(far, part) == 1 else 1
        y_copy(far, part, first).start()
        y_copy(far, part, 1 - first).start()

    def y_pass(far, part):
        way = 0 if pass_step(far, part) == 1 else 1
        y_arrival(far, part, way).wait_recv()
        y_copy(far, part, 2).start()

    def y_rest(far, parts):
        for part in parts:
            y_arrival(far, part, 1 if pass_step(far, part) == 1 else 0).wait_recv()
            y_arrival(far, part, 2).wait_recv()

    def far_copy(part, slot):
        ref = token_part(part, slot)
        return remote(ref, ref, z_sems, (part,), tp_of(y, 1 - hi))

    def far_pass(part):
        far_copy(part, t_far).wait_recv()
        if part + 3 < PARTS:
            far_copy(part + 3, t).start()
        y_send(1, part)

    weights = (w_s, w_o)

    def wz_copy(m, way, step, source):
        ref = weights[m].at[source * 8 + x * 2 + core]
        return remote(
            ref, ref, wz_sems, (m, way, step),
            grp_of((lo + (1, 3)[way]) % 4, x, core),
        )

    def wz_first(m):
        wz_copy(m, 0, 0, lo).start(lo < 3)
        wz_copy(m, 1, 0, lo).start(lo > 0)

    def wz_step(m, step):
        for way in (0, 1):
            source = (lo + (step + 1) * (-1, 1)[way] + 4) % 4
            came = (lo > step, lo < 3 - step)[way]
            wz_copy(m, way, step, source).wait_recv(came)
            if step < 2:
                wz_copy(m, way, step + 1, source).start(came & (lo < 3, lo > 0)[way])
            for d in (2, 1, 3):
                wx_copy(m, 1 + 3 * way + step, d, x).start(came)
            wc_copy(m, 1 + 3 * way + step, 0, core).start(came)

    def line(b):
        if b == 0:
            return lo, None
        step = (b - 1) % 3
        way = (b - 1) // 3
        return (lo + (step + 1) * (-1, 1)[way] + 4) % 4, (lo > step, lo < 3 - step)[way]

    def w_pass(m, b):
        for d in (1, 3, 2):
            wx_copy(m, b, d, (x - d + 4) % 4).wait_recv(line(b)[1])
            wc_copy(m, b, d, core).start(line(b)[1])

    def w_done(m):
        for b in range(7):
            for d in range(4):
                wc_copy(m, b, d, 1 - core).wait_recv(line(b)[1])

    def wx_copy(m, b, d, x_):
        ref = weights[m].at[line(b)[0] * 8 + x_ * 2 + core]
        return remote(
            ref, ref, wx_sems, (m, b, d), grp_of(lo, (x + d) % 4, core)
        )

    def wc_copy(m, b, d, c_):
        ref = weights[m].at[line(b)[0] * 8 + ((x - d + 4) % 4) * 2 + c_]
        return remote(
            ref, ref, wc_sems, (m, b, d), grp_of(lo, x, 1 - core)
        )

    def w_spread(m, b):
        for d in (2, 1, 3):
            wx_copy(m, b, d, x).start()
        wc_copy(m, b, 0, core).start()

    def ar_copy(which, buf, j, slot):
        ref = buf.at[slot]
        return remote(
            ref, ref, ar_sems, (which, j),
            tp_of((y + j // 2) % 4, (hi + j % 2) % 2),
        )

    def ar_start(which, buf):
        for j in (5, 7, 3, 4, 1, 2, 6):
            ar_copy(which, buf, j, t).start()

    def ar_finish(which, buf):
        for j in range(1, 8):
            ar_copy(which, buf, j, ((y - j // 2 + 4) % 4) * 2 + (hi + j % 2) % 2).wait_recv()
        total = buf[0]
        for j in range(1, 8):
            total = total + buf[j]
        return total

    def ig_copy(i, l_, x_, c_):
        if i == 0:
            ref, device = ig.at[lo, x * 2 + c_], grp_of(lo, x, 1 - core)
        elif i < 4:
            ref, device = ig.at[lo, pl.ds(x_ * 2, 2)], grp_of(lo, (x + i) % 4, core)
        else:
            ref, device = ig.at[l_], grp_of((lo + i - 3) % 4, x, core)
        return remote(ref, ref, ig_sems, (i,), device)

    def multiply(h_ref, buf, w_ref, half_of):
        def body(i, carry):
            k = ((y + i) % 4) * 2 + half_of
            piece = w_ref[pl.ds(4 * k, 4)].reshape(512, COLS)
            h_ref[...] += jnp.dot(buf[k], piece, preferred_element_type=F32)
            return carry

        lax.fori_loop(0, 4, body, 0)

    def turn(half_of):
        def body(i, carry):
            k = ((y + i) % 4) * 2 + half_of
            turned = a_e[k].T
            for b in range(4):
                at = (half_of * 2 + b // 2) * 8 + (b % 2) * 4 + (y + i) % 4
                a_t[at] = turned[b * 128 : b * 128 + 128, :]
            return carry

        lax.fori_loop(0, 4, body, 0)

    for i in (0, 1):
        locals_[i].wait()
    wz_first(0)
    for part in range(4):
        y_send(0, part)
        if part < 3:
            far_copy(part, t).start()
    w_spread(0, 0)
    for i in (2, 3, 4):
        locals_[i].wait()
    for part in (4, 5, 6):
        y_send(0, part)
    w_spread(1, 0)
    wz_step(0, 0)
    for i in (5, 6, 7):
        locals_[i].wait()
    h_s[...] = r_s[...].astype(F32)
    h_e[...] = r_e[...].astype(F32)
    y_pass(0, 0)
    y_pass(0, 1)
    far_pass(0)
    y_pass(0, 2)
    y_pass(0, 3)
    wz_step(0, 1)
    far_pass(1)
    wz_step(0, 2)
    wz_first(1)
    w_pass(0, 0)
    w_pass(0, 1)
    w_pass(0, 4)
    far_pass(2)
    y_pass(0, 4)
    y_pass(0, 5)
    y_pass(0, 6)
    w_pass(0, 2)
    w_pass(0, 5)
    far_pass(3)
    w_pass(0, 3)
    w_pass(0, 6)
    w_pass(1, 0)
    y_pass(1, 0)
    y_pass(1, 1)
    far_pass(4)
    wz_step(1, 0)
    w_done(0)
    y_rest(0, range(4))
    multiply(h_s, a_s, w_s, hi)
    y_pass(1, 2)
    y_pass(1, 3)
    far_pass(5)
    wz_step(1, 1)
    for b in (1, 4):
        w_pass(1, b)
    y_rest(1, range(4))
    multiply(h_s, a_s, w_s, 1 - hi)

    ar_s[t] = jnp.zeros((8, 128), F32)
    for b in range(4):
        ar_s[t, b : b + 1, :] = square_rows(h_s, b)
    ar_start(0, ar_s)
    y_pass(1, 4)
    far_pass(6)
    wz_step(1, 2)
    y_pass(1, 5)
    y_rest(0, (4, 5, 6))
    turn(hi)
    for b in (2, 5):
        w_pass(1, b)
    gain = gain_ref[...].astype(F32)

    factor_s = lax.rsqrt(ar_finish(0, ar_s) / WIDTH + EPS)
    ar_p[t] = jnp.zeros((8, 128), F32)
    for s in range(2):
        count = pass_len[s]
        total = jnp.zeros((1, COLS), F32)
        for b in range(2):
            rows = lax.broadcasted_iota(jnp.int32, (128, 128), 0) + b * 128
            col = spread_rows(factor_s[2 * s + b : 2 * s + b + 1, :])
            col = jnp.where(rows < count, col, 0.0)
            part = h_s[pl.ds((2 * s + b) * 128, 128), :] * lanes4(col)
            total = total + jnp.sum(part, axis=0, keepdims=True)
        total = total * gain / jnp.full((1, COLS), count, jnp.int32).astype(F32)
        pool_s[s : s + 1, :] = total
        square = jnp.sum(total * total, axis=1, keepdims=True)
        ar_p[t, s : s + 1, :] = jnp.broadcast_to(square, (1, 128))
    ar_start(1, ar_p)
    y_pass(1, 6)
    for b in (3, 6):
        w_pass(1, b)
    w_done(1)
    multiply(h_e, a_e, w_o, hi)
    norm_s = lax.rsqrt(ar_finish(1, ar_p) / WIDTH + EPS)
    for s in range(2):
        row = (pool_s[s : s + 1, :] * lanes4(norm_s[s : s + 1, :])).astype(BF16).astype(F32)
        pool_s[s : s + 1, :] = row
        for b in range(4):
            ig[lo, x * 2 + core, 4 * s + b : 4 * s + b + 1, :] = row[:, b * 128 : b * 128 + 128]
    index_ref[...] = pool_s[0:2, :].astype(BF16)
    ig_copy(0, lo, x, core).start()
    ig_copy(0, lo, x, 1 - core).wait_recv()
    for i in (2, 1, 3):
        ig_copy(i, lo, x, core).start()

    y_rest(1, (4, 5, 6))
    multiply(h_e, a_e, w_o, 1 - hi)
    ar_e[t] = jnp.zeros((8, 128), F32)
    for b in range(3):
        ar_e[t, b : b + 1, :] = square_rows(h_e, b)
    ar_start(2, ar_e)
    for i in (1, 2, 3):
        ig_copy(i, lo, (x - i + 4) % 4, core).wait_recv()
    for i in (5, 4, 6):
        ig_copy(i, lo, x, core).start()
    turn(1 - hi)

    factor = lax.rsqrt(ar_finish(2, ar_e) / WIDTH + EPS)
    f_row[...] = factor
    for b in range(3):
        fcol[pl.ds(b * 128, 128), :] = spread_rows(factor[b : b + 1, :])
    for r, (first, count) in enumerate(((0, 64), (64, 64), (128, 128), (256, 128))):
        part = h_e[pl.ds(first, count), :] * lanes4(fcol[pl.ds(first, count), :])
        vec[r : r + 1, :] = jnp.sum(part, axis=0, keepdims=True) * gain / count
    for i in (4, 5, 6):
        ig_copy(i, (lo - i + 3 + 4) % 4, x, core).wait_recv()
    for r in range(2):
        for j in range(8):
            name = neg_ids[r, j]
            owner = block_owner[name // 2]
            tile = ig[owner // 8, owner % 8]
            piece = jnp.where(name % 2 == 0, tile[0:4, :], tile[4:8, :])
            at = 8 + 8 * r + j
            for b in range(4):
                vec[at : at + 1, b * 128 : b * 128 + 128] = piece[b : b + 1, :]

    nt = (((1,), (1,)), ((), ()))
    vec_g[...] = vec[0:32, :] * gain
    sims = lax.dot_general(vec_g[...], h_e[...], nt, precision=HI, preferred_element_type=F32)
    gram = lax.dot_general(vec[0:8, :], vec[...], nt, precision=HI, preferred_element_type=F32)
    first = lax.broadcasted_iota(jnp.int32, (1, 128), 1) < 64
    ar_g[t, 0:8, :] = jnp.where(first, sims[8:16, 0:128], sims[16:24, 0:128])
    ar_g[t, 8:16, :] = jnp.zeros((8, 128), F32)
    ar_g[t, 8:9, :] = jnp.where(first, sims[0:1, 0:128], sims[1:2, 0:128])
    ar_g[t, 9:10, :] = jnp.where(first, sims[2:3, 0:128], sims[3:4, 0:128])
    ar_g[t, 10:11, :] = sims[0:1, 128:256]
    ar_g[t, 11:12, :] = sims[2:3, 128:256]
    ar_g[t, 12:13, :] = sims[1:2, 256:384]
    ar_g[t, 13:14, :] = sims[3:4, 256:384]
    ar_g[t, 16:24, :] = gram
    left = list(sent)
    sent.clear()
    ar_start(3, ar_g)
    for copy in left:
        copy.wait_send()
    both = ar_finish(3, ar_g)

    gram = both[16:24, :]
    row = lax.broadcasted_iota(jnp.int32, (8, 128), 0)
    lane = lax.broadcasted_iota(jnp.int32, (8, 128), 1)
    diag = jnp.where((lane == row) & (row < 4), gram, 0.0)
    norm_row = lax.rsqrt(jnp.sum(diag, axis=1, keepdims=True) / WIDTH + EPS)
    norm_lane = lax.rsqrt(jnp.sum(diag, axis=0, keepdims=True) / WIDTH + EPS)
    norm_lane = jnp.where(lane < 4, norm_lane, 1.0)
    unit = gram * norm_row * norm_lane
    is_pos = (lane == row + 2) & (row < 2)
    is_neg = (lane >= 8 + 8 * row) & (lane < 16 + 8 * row) & (row < 2)
    pos = jnp.sum(jnp.where(is_pos, unit, 0.0), axis=1, keepdims=True) * SCALE
    exp_neg = jnp.where(is_neg, jnp.exp(jnp.where(is_neg, unit, 0.0) * SCALE), 0.0)
    exp_pos = jnp.exp(pos)
    total = exp_pos + jnp.sum(exp_neg, axis=1, keepdims=True)
    terms = jnp.where(row < 2, jnp.log(total) - pos, 0.0)
    loss = jnp.sum(terms, axis=0, keepdims=True)
    d_pos = jnp.where(is_pos, exp_pos / total - 1.0, 0.0)
    pos_lane = jnp.sum(d_pos, axis=0, keepdims=True)
    pos_row = jnp.sum(jnp.where(lane == row, pos_lane, 0.0), axis=1, keepdims=True)
    coef = d_pos + exp_neg / total
    coef = coef + jnp.where((lane == row - 2) & (row < 4), pos_row, 0.0)
    coef = coef * SCALE
    back = jnp.sum(coef * unit, axis=1, keepdims=True) / WIDTH
    coef = norm_row * (coef * norm_lane - jnp.where(lane == row, back * norm_row, 0.0))
    coef = jnp.where(row < 4, coef, 0.0)
    coef = coef / jnp.where(row < 2, 64.0, 128.0)

    l_c[core] = jnp.broadcast_to(loss, (8, 128))
    pair_loss = remote(
        l_c.at[core], l_c.at[core], ls_sems, (0,), grp_of(lo, x, 1 - core)
    )
    pair_loss.start()

    s_full[8:16, 0:128] = both[0:8, :]
    s_full[16:24, 0:128] = both[0:8, :]
    s_full[0:2, 0:128] = jnp.broadcast_to(both[8:9, :], (2, 128))
    s_full[2:4, 0:128] = jnp.broadcast_to(both[9:10, :], (2, 128))
    s_full[0:1, 128:256] = both[10:11, :]
    s_full[2:3, 128:256] = both[11:12, :]
    s_full[1:2, 256:384] = both[12:13, :]
    s_full[3:4, 256:384] = both[13:14, :]
    inner = jnp.dot(coef, s_full[...], precision=HI, preferred_element_type=F32)
    urow[...] = jnp.dot(coef, vec[...], precision=HI, preferred_element_type=F32) * gain
    wanted = (
        ((row == 0) & (lane < 64)) | ((row == 1) & (lane >= 64)),
        row == 2,
        row == 3,
    )
    for b in range(3):
        line = jnp.sum(
            jnp.where(wanted[b], inner[:, b * 128 : b * 128 + 128], 0.0), axis=0, keepdims=True
        )
        f = f_row[b : b + 1, :]
        gcol[pl.ds(b * 128, 128), :] = spread_rows(line * f * f / WIDTH)
    for r, (first, count) in enumerate(((0, 64), (64, 64), (128, 128), (256, 128))):
        at = pl.ds(first, count)
        part = urow[r : r + 1, :] - h_e[at, :] * lanes4(gcol[at, :])
        dh[at, :] = (lanes4(fcol[at, :]) * part).astype(BF16)

    def pc_copy(i, x_):
        return remote(
            psend.at[x_], precv.at[x_], pc_sems, (i,), grp_of(lo, x, 1 - core)
        )

    up = (1, -1, 1, -1)
    line_of = (3 * (1 - lo // 2), 2 - lo // 2, lo + 1 - 2 * (lo % 2), lo)

    def px_copy(stage, side, d):
        at = stage + side
        return remote(
            xsend.at[at, d], xrecv.at[at, d], px_sems, (at, d),
            grp_of(lo, (x + (up[d], 1, -1)[at] + 4) % 4, core),
        )

    def pz_copy(k):
        d = (line_of[k] - lo + 4) % 4
        return remote(
            zsend.at[k], zrecv.at[d], pz_sems, (d,), grp_of(line_of[k], x, core)
        )

    def pz_arrival(d):
        return remote(zsend.at[d], zrecv.at[d], pz_sems, (d,), grp_of(lo, x, core))

    turns = (2, 1, 3, 0)

    def part_of(x_, c_):
        rows = a_t[pl.ds((x_ * 2 + c_) * 4, 4)].reshape(512, ETOK)
        part = jnp.dot(rows, dh[...], preferred_element_type=F32)
        return part.reshape(4, 128, COLS)

    def give(i):
        x_ = (x + turns[i]) % 4
        psend[x_] = part_of(x_, 1 - core).astype(BF16)
        pc_copy(i, x_).start()

    def keep(i):
        x_ = (x + turns[i]) % 4
        own[x_] = part_of(x_, core)

    def pair_sum(x_, d):
        l_ = line_of[d]
        return own[x_, l_] + precv[x_, l_].astype(F32)

    def direct(d):
        side = 0 if up[d] == -1 else 1
        xsend[1 + side, d] = pair_sum((x + (1, 3)[side]) % 4, d).astype(BF16)
        px_copy(1, side, d).start()

    def relay(d):
        side = 0 if up[d] == 1 else 1
        px_copy(0, 0, d).wait_recv()
        total = pair_sum((x + (1, 3)[side]) % 4, d) + xrecv[0, d].astype(F32)
        xsend[1 + side, d] = total.astype(BF16)
        px_copy(1, side, d).start()

    give(0)
    keep(0)
    give(1)
    pair_loss.wait_recv()
    l_x[x] = l_c[0] + l_c[1]

    def lx_copy(d, slot):
        return remote(
            l_x.at[slot], l_x.at[slot], ls_sems, (d,), grp_of(lo, (x + d) % 4, core)
        )

    def lz_copy(d, slot):
        return remote(
            l_z.at[slot], l_z.at[slot], ls_sems, (3 + d,),
            grp_of((lo + d) % 4, x, core),
        )

    for d in (1, 2, 3):
        lx_copy(d, x).start()
    pc_copy(0, x).wait_recv()
    for d in range(4):
        xsend[0, d] = pair_sum((x + 2) % 4, d).astype(BF16)
        px_copy(0, 0, d).start()
    keep(1)
    give(2)
    keep(2)
    give(3)
    pc_copy(1, x).wait_recv()
    pc_copy(2, x).wait_recv()
    left = list(sent[:8])
    del sent[:8]
    for copy in left:
        copy.wait_send()
    relay(0)
    relay(1)
    direct(1)
    direct(0)
    keep(3)
    for d in (1, 2, 3):
        lx_copy(d, (x - d + 4) % 4).wait_recv()
    l_z[lo] = (l_x[0] + l_x[1]) + (l_x[2] + l_x[3])
    for d in (1, 2, 3):
        lz_copy(d, lo).start()
    relay(2)
    direct(2)
    direct(3)
    relay(3)
    pc_copy(3, x).wait_recv()
    for d in range(4):
        total = pair_sum(x, d)
        for side in (0, 1):
            px_copy(1, side, d).wait_recv()
        total = total + (xrecv[1, d].astype(F32) + xrecv[2, d].astype(F32))
        if d == 3:
            grad_ref[...] = total
        else:
            zsend[d] = total.astype(BF16)
            pz_copy(d).start()
    for d in (1, 2, 3):
        lz_copy(d, (lo - d + 4) % 4).wait_recv()
    loss_ref[...] = ((l_z[0] + l_z[1]) + (l_z[2] + l_z[3]))[0:1, 0:1] / 64.0
    for d in (1, 3, 2):
        pz_arrival(d).wait_recv()
    grad_ref[...] += (zrecv[1].astype(F32) + zrecv[2].astype(F32)) + zrecv[3].astype(F32)

    for copy in sent:
        copy.wait_send()


def shards(
    q_attn, q_resid, p_attn, p_resid, w_out, w_snap, norm_gain, pass_attn, pass_resid,
    pass_len, block_owner, neg_ids,
):
    hbm = pl.BlockSpec(memory_space=pl.ANY)
    vmem = pl.BlockSpec(memory_space=pltpu.VMEM)
    smem = pl.BlockSpec(memory_space=pltpu.SMEM)
    dma = pltpu.SemaphoreType.DMA

    def both(shape):
        return (dma(shape), dma(shape))

    loss, grad, index = pl.pallas_call(
        kernel,
        out_shape=(
            jax.ShapeDtypeStruct((1, 1), F32),
            jax.ShapeDtypeStruct((128, COLS), F32),
            jax.ShapeDtypeStruct((2, COLS), BF16),
        ),
        in_specs=[hbm] * 6 + [vmem] + [hbm] * 2 + [smem] * 3,
        out_specs=(vmem, vmem, vmem),
        scratch_shapes=[
            pltpu.VMEM((8, STOK, COLS), BF16),
            pltpu.VMEM((8, ETOK, COLS), BF16),
            pltpu.VMEM((32, 128, COLS), BF16),
            pltpu.VMEM((32, 128, COLS), BF16),
            pltpu.VMEM((STOK, COLS), BF16),
            pltpu.VMEM((ETOK, COLS), BF16),
            pltpu.VMEM((STOK, COLS), F32),
            pltpu.VMEM((ETOK, COLS), F32),
            pltpu.VMEM((32, 128, ETOK), BF16),
            pltpu.VMEM((8, 8, 128), F32),
            pltpu.VMEM((8, 8, 128), F32),
            pltpu.VMEM((8, 8, 128), F32),
            pltpu.VMEM((8, 24, 128), F32),
            pltpu.VMEM((4, 8, 8, 128), F32),
            pltpu.VMEM((8, COLS), F32),
            pltpu.VMEM((128, COLS), F32),
            pltpu.VMEM((32, COLS), F32),
            pltpu.VMEM((128, ETOK), F32),
            pltpu.VMEM((ETOK, 128), F32),
            pltpu.VMEM((ETOK, 128), F32),
            pltpu.VMEM((8, 128), F32),
            pltpu.VMEM((8, COLS), F32),
            pltpu.VMEM((ETOK, COLS), BF16),
            pltpu.VMEM((4, 4, 128, COLS), F32),
            pltpu.VMEM((4, 4, 128, COLS), BF16),
            pltpu.VMEM((4, 4, 128, COLS), BF16),
            pltpu.VMEM((3, 4, 128, COLS), BF16),
            pltpu.VMEM((3, 4, 128, COLS), BF16),
            pltpu.VMEM((4, 128, COLS), BF16),
            pltpu.VMEM((4, 128, COLS), BF16),
            pltpu.VMEM((2, 8, 128), F32),
            pltpu.VMEM((4, 8, 128), F32),
            pltpu.VMEM((4, 8, 128), F32),
            dma((8,)),
            both((2, PARTS, 3)),
            both((PARTS,)),
            both((2, 2, 3)),
            both((2, 7, 4)),
            both((2, 7, 4)),
            both((4, 8)),
            both((7,)),
            both((4,)),
            both((3, 4)),
            both((4,)),
            both((7,)),
        ],
        compiler_params=pltpu.CompilerParams(
            collective_id=0, has_side_effects=True, vmem_limit_bytes=56 * 2**20
        ),
    )(
        q_attn.reshape(128, COLS),
        q_resid.reshape(128, COLS),
        p_attn.reshape(256, COLS),
        p_resid.reshape(256, COLS),
        w_out,
        w_snap,
        norm_gain.reshape(1, COLS),
        pass_attn.reshape(STOK, COLS),
        pass_resid.reshape(STOK, COLS),
        pass_len,
        block_owner,
        neg_ids,
    )
    return (loss[0, 0], grad, index)


def solution(mesh):
    placed = (
        P("grp", None, "tp"),
        P("grp", None, "tp"),
        P("grp", None, "tp"),
        P("grp", None, "tp"),
        P("grp", "tp"),
        P("grp", "tp"),
        P("tp"),
        P("grp", None, "tp"),
        P("grp", None, "tp"),
        P("grp"),
        P(),
        P("grp", None),
    )
    return jax.shard_map(
        shards,
        mesh=mesh,
        in_specs=placed,
        out_specs=(P(), P("grp", "tp"), P("grp", "tp")),
        check_vma=False,
    )
```

```python
import functools

import jax
import jax.numpy as jnp
from jax import lax
from jax.experimental import pallas as pl
from jax.experimental.pallas import tpu as pltpu
from jax.sharding import PartitionSpec as P

EPS = 1e-06
TEMP = 0.05
WIDTH = 4096
COLS = 512
STOK = 512
ETOK = 384
SCALE = 1.0 / (WIDTH * TEMP)
MESH = pl.DeviceIdType.MESH
HI = lax.Precision.HIGHEST
F32 = jnp.float32
BF16 = jnp.bfloat16
PARTS = 7


class Copy:
    def __init__(self, sent, src, dst, sems, at, device):
        self.sent = sent
        self.key = (id(sems), at)
        self.copy = pltpu.make_async_remote_copy(
            src_ref=src, dst_ref=dst, send_sem=sems[0].at[at], recv_sem=sems[1].at[at],
            device_id=device, device_id_type=MESH,
        )

    def start(self, when=None):
        self.when = when
        self.sent.append(self)
        self.guard(when, self.copy.start)

    def wait_recv(self, when=None):
        self.guard(when, self.copy.wait_recv)

    def wait_send(self):
        self.guard(self.when, self.copy.wait_send)

    def guard(self, when, action):
        if when is None:
            action()
        else:
            pl.when(when)(action)


def lanes4(col):
    return jnp.concatenate([col, col, col, col], axis=1)


def spread_rows(row):
    return jnp.broadcast_to(row, (128, 128)).T


def square_rows(h_ref, block):
    part = h_ref[pl.ds(block * 128, 128), :]
    part = part * part
    part = (part[:, 0:128] + part[:, 128:256]) + (part[:, 256:384] + part[:, 384:512])
    return jnp.sum(part.T, axis=0, keepdims=True)


def kernel(
    q_attn, q_resid, p_attn, p_resid, w_out, w_snap, gain_ref, s_attn, s_resid,
    pass_len, block_owner, neg_ids,
    loss_ref, grad_ref, index_ref,
    a_s, a_e, w_s, w_o, r_s, r_e, h_s, h_e, a_t,
    ar_s, ar_p, ar_e, ar_g, ig, pool_s, vec, vec_g, s_full, fcol, gcol, f_row, urow, dh,
    own, psend, precv, xsend, xrecv, zsend, zrecv, l_c, l_x, l_z,
    loc, y_sems, z_sems, wz_sems, wx_sems, wc_sems, ar_sems, ig_sems, pc_sems, px_sems, pz_sems,
    ls_sems,
):
    grp = lax.axis_index("grp")
    t = lax.axis_index("tp")
    core = grp % 2
    x = (grp // 2) % 4
    lo = grp // 8
    y = t // 2
    hi = t % 2
    t_far = y * 2 + (1 - hi)

    def grp_of(l_, x_, c_):
        return (l_ * 8 + x_ * 2 + c_, t)

    def tp_of(y_, h_):
        return (grp, y_ * 2 + h_)

    sent = []

    def remote(src, dst, sems, at, device):
        return Copy(sent, src, dst, sems, at, device)

    locals_ = [
        pltpu.make_async_copy(w_snap, w_s.at[grp], loc.at[0]),
        pltpu.make_async_copy(s_attn, a_s.at[t], loc.at[1]),
        pltpu.make_async_copy(w_out, w_o.at[grp], loc.at[2]),
        pltpu.make_async_copy(q_attn, a_e.at[t, pl.ds(0, 128)], loc.at[3]),
        pltpu.make_async_copy(p_attn, a_e.at[t, pl.ds(128, 256)], loc.at[4]),
        pltpu.make_async_copy(s_resid, r_s, loc.at[5]),
        pltpu.make_async_copy(q_resid, r_e.at[pl.ds(0, 128)], loc.at[6]),
        pltpu.make_async_copy(p_resid, r_e.at[pl.ds(128, 256)], loc.at[7]),
    ]
    for copy in locals_:
        copy.start()

    barrier = pltpu.get_barrier_semaphore()
    peers = [grp_of(lo, x, 1 - core)]
    for d in (1, 2, 3):
        peers.append(grp_of(lo, (x + d) % 4, core))
        peers.append(grp_of((lo + d) % 4, x, core))
        peers.append(tp_of((y + d) % 4, hi))
    peers.append(tp_of(y, 1 - hi))
    for peer in peers:
        pl.semaphore_signal(barrier, inc=1, device_id=peer, device_id_type=MESH)
    vec[...] = jnp.zeros_like(vec)
    s_full[...] = jnp.zeros_like(s_full)
    pl.semaphore_wait(barrier, len(peers))

    def token_part(part, slot):
        if part < 4:
            return a_s.at[slot, pl.ds(part * 128, 128)]
        return a_e.at[slot, pl.ds((part - 4) * 128, 128)]

    def pass_step(far, part):
        return 1 if (part + far) % 2 == 0 else -1

    def y_copy(far, part, way):
        step = (1, -1, pass_step(far, part))[way]
        row = y if way < 2 else (y - step + 4) % 4
        ref = token_part(part, row * 2 + (hi if far == 0 else 1 - hi))
        return remote(ref, ref, y_sems, (far, part, way), tp_of((y + step + 4) % 4, hi))

    def y_arrival(far, part, way):
        step = (1, -1, 2 * pass_step(far, part))[way]
        ref = token_part(part, ((y - step + 4) % 4) * 2 + (hi if far == 0 else 1 - hi))
        return remote(ref, ref, y_sems, (far, part, way), tp_of(y, hi))

    def y_send(far, part):
        first = 0 if pass_step(far, part) == 1 else 1
        y_copy(far, part, first).start()
        y_copy(far, part, 1 - first).start()

    def y_pass(far, part):
        way = 0 if pass_step(far, part) == 1 else 1
        y_arrival(far, part, way).wait_recv()
        y_copy(far, part, 2).start()

    def y_rest(far, parts):
        for part in parts:
            y_arrival(far, part, 1 if pass_step(far, part) == 1 else 0).wait_recv()
            y_arrival(far, part, 2).wait_recv()

    def far_copy(part, slot):
        ref = token_part(part, slot)
        return remote(ref, ref, z_sems, (part,), tp_of(y, 1 - hi))

    def far_pass(part):
        far_copy(part, t_far).wait_recv()
        if part + 3 < PARTS:
            far_copy(part + 3, t).start()
        y_send(1, part)

    weights = (w_s, w_o)

    def wz_copy(m, way, step, source):
        ref = weights[m].at[source * 8 + x * 2 + core]
        return remote(
            ref, ref, wz_sems, (m, way, step),
            grp_of((lo + (1, 3)[way]) % 4, x, core),
        )

    def wz_first(m):
        wz_copy(m, 0, 0, lo).start(lo < 3)
        wz_copy(m, 1, 0, lo).start(lo > 0)

    def wz_step(m, step):
        for way in (0, 1):
            source = (lo + (step + 1) * (-1, 1)[way] + 4) % 4
            came = (lo > step, lo < 3 - step)[way]
            wz_copy(m, way, step, source).wait_recv(came)
            if step < 2:
                wz_copy(m, way, step + 1, source).start(came & (lo < 3, lo > 0)[way])
            for d in (2, 1, 3):
                wx_copy(m, 1 + 3 * way + step, d, x).start(came)
            wc_copy(m, 1 + 3 * way + step, 0, core).start(came)

    def line(b):
        if b == 0:
            return lo, None
        step = (b - 1) % 3
        way = (b - 1) // 3
        return (lo + (step + 1) * (-1, 1)[way] + 4) % 4, (lo > step, lo < 3 - step)[way]

    def w_pass(m, b):
        for d in (1, 3, 2):
            wx_copy(m, b, d, (x - d + 4) % 4).wait_recv(line(b)[1])
            wc_copy(m, b, d, core).start(line(b)[1])

    def w_done(m):
        for b in range(7):
            for d in range(4):
                wc_copy(m, b, d, 1 - core).wait_recv(line(b)[1])

    def wx_copy(m, b, d, x_):
        ref = weights[m].at[line(b)[0] * 8 + x_ * 2 + core]
        return remote(
            ref, ref, wx_sems, (m, b, d), grp_of(lo, (x + d) % 4, core)
        )

    def wc_copy(m, b, d, c_):
        ref = weights[m].at[line(b)[0] * 8 + ((x - d + 4) % 4) * 2 + c_]
        return remote(
            ref, ref, wc_sems, (m, b, d), grp_of(lo, x, 1 - core)
        )

    def w_spread(m, b):
        for d in (2, 1, 3):
            wx_copy(m, b, d, x).start()
        wc_copy(m, b, 0, core).start()

    def ar_copy(which, buf, j, slot):
        ref = buf.at[slot]
        return remote(
            ref, ref, ar_sems, (which, j),
            tp_of((y + j // 2) % 4, (hi + j % 2) % 2),
        )

    def ar_start(which, buf):
        for j in (5, 7, 3, 4, 1, 2, 6):
            ar_copy(which, buf, j, t).start()

    def ar_finish(which, buf):
        for j in range(1, 8):
            ar_copy(which, buf, j, ((y - j // 2 + 4) % 4) * 2 + (hi + j % 2) % 2).wait_recv()
        total = buf[0]
        for j in range(1, 8):
            total = total + buf[j]
        return total

    def ig_copy(i, l_, x_, c_):
        if i == 0:
            ref, device = ig.at[lo, x * 2 + c_], grp_of(lo, x, 1 - core)
        elif i < 4:
            ref, device = ig.at[lo, pl.ds(x_ * 2, 2)], grp_of(lo, (x + i) % 4, core)
        else:
            ref, device = ig.at[l_], grp_of((lo + i - 3) % 4, x, core)
        return remote(ref, ref, ig_sems, (i,), device)

    def multiply(h_ref, buf, w_ref, half_of):
        def body(i, carry):
            k = ((y + i) % 4) * 2 + half_of
            piece = w_ref[pl.ds(4 * k, 4)].reshape(512, COLS)
            h_ref[...] += jnp.dot(buf[k], piece, preferred_element_type=F32)
            return carry

        lax.fori_loop(0, 4, body, 0)

    def turn(half_of):
        def body(i, carry):
            k = ((y + i) % 4) * 2 + half_of
            turned = a_e[k].T
            for b in range(4):
                at = (half_of * 2 + b // 2) * 8 + (b % 2) * 4 + (y + i) % 4
                a_t[at] = turned[b * 128 : b * 128 + 128, :]
            return carry

        lax.fori_loop(0, 4, body, 0)

    for i in (0, 1):
        locals_[i].wait()
    wz_first(0)
    for part in range(4):
        y_send(0, part)
        if part < 3:
            far_copy(part, t).start()
    w_spread(0, 0)
    for i in (2, 3, 4):
        locals_[i].wait()
    for part in (4, 5, 6):
        y_send(0, part)
    w_spread(1, 0)
    wz_step(0, 0)
    for i in (5, 6, 7):
        locals_[i].wait()
    h_s[...] = r_s[...].astype(F32)
    h_e[...] = r_e[...].astype(F32)
    y_pass(0, 0)
    y_pass(0, 1)
    far_pass(0)
    y_pass(0, 2)
    y_pass(0, 3)
    wz_step(0, 1)
    far_pass(1)
    wz_step(0, 2)
    wz_first(1)
    w_pass(0, 0)
    w_pass(0, 1)
    w_pass(0, 4)
    far_pass(2)
    y_pass(0, 4)
    y_pass(0, 5)
    y_pass(0, 6)
    w_pass(0, 2)
    w_pass(0, 5)
    far_pass(3)
    w_pass(0, 3)
    w_pass(0, 6)
    w_pass(1, 0)
    y_pass(1, 0)
    y_pass(1, 1)
    far_pass(4)
    wz_step(1, 0)
    w_done(0)
    y_rest(0, range(4))
    multiply(h_s, a_s, w_s, hi)
    y_pass(1, 2)
    y_pass(1, 3)
    far_pass(5)
    wz_step(1, 1)
    for b in (1, 4):
        w_pass(1, b)
    y_rest(1, range(4))
    multiply(h_s, a_s, w_s, 1 - hi)

    ar_s[t] = jnp.zeros((8, 128), F32)
    for b in range(4):
        ar_s[t, b : b + 1, :] = square_rows(h_s, b)
    ar_start(0, ar_s)
    y_pass(1, 4)
    far_pass(6)
    wz_step(1, 2)
    y_pass(1, 5)
    y_rest(0, (4, 5, 6))
    turn(hi)
    for b in (2, 5):
        w_pass(1, b)
    gain = gain_ref[...].astype(F32).reshape(1, COLS)

    factor_s = lax.rsqrt(ar_finish(0, ar_s) / WIDTH + EPS)
    ar_p[t] = jnp.zeros((8, 128), F32)
    for s in range(2):
        count = pass_len[s]
        total = jnp.zeros((1, COLS), F32)
        for b in range(2):
            rows = lax.broadcasted_iota(jnp.int32, (128, 128), 0) + b * 128
            col = spread_rows(factor_s[2 * s + b : 2 * s + b + 1, :])
            col = jnp.where(rows < count, col, 0.0)
            part = h_s[pl.ds((2 * s + b) * 128, 128), :] * lanes4(col)
            total = total + jnp.sum(part, axis=0, keepdims=True)
        total = total * gain / jnp.full((1, COLS), count, jnp.int32).astype(F32)
        pool_s[s : s + 1, :] = total
        square = jnp.sum(total * total, axis=1, keepdims=True)
        ar_p[t, s : s + 1, :] = jnp.broadcast_to(square, (1, 128))
    ar_start(1, ar_p)
    y_pass(1, 6)
    for b in (3, 6):
        w_pass(1, b)
    w_done(1)
    multiply(h_e, a_e, w_o, hi)
    norm_s = lax.rsqrt(ar_finish(1, ar_p) / WIDTH + EPS)
    for s in range(2):
        row = (pool_s[s : s + 1, :] * lanes4(norm_s[s : s + 1, :])).astype(BF16).astype(F32)
        pool_s[s : s + 1, :] = row
        for b in range(4):
            ig[lo, x * 2 + core, 4 * s + b : 4 * s + b + 1, :] = row[:, b * 128 : b * 128 + 128]
    index_ref[...] = pool_s[0:2, :].astype(BF16)
    ig_copy(0, lo, x, core).start()
    ig_copy(0, lo, x, 1 - core).wait_recv()
    for i in (2, 1, 3):
        ig_copy(i, lo, x, core).start()

    y_rest(1, (4, 5, 6))
    multiply(h_e, a_e, w_o, 1 - hi)
    ar_e[t] = jnp.zeros((8, 128), F32)
    for b in range(3):
        ar_e[t, b : b + 1, :] = square_rows(h_e, b)
    ar_start(2, ar_e)
    for i in (1, 2, 3):
        ig_copy(i, lo, (x - i + 4) % 4, core).wait_recv()
    for i in (5, 4, 6):
        ig_copy(i, lo, x, core).start()
    turn(1 - hi)

    for i in (4, 5, 6):
        ig_copy(i, (lo - i + 3 + 4) % 4, x, core).wait_recv()
    for r in range(2):
        for j in range(8):
            name = neg_ids[r, j]
            owner = block_owner[name // 2]
            tile = ig[owner // 8, owner % 8]
            piece = jnp.where(name % 2 == 0, tile[0:4, :], tile[4:8, :])
            at = 8 + 8 * r + j
            for b in range(4):
                vec[at : at + 1, b * 128 : b * 128 + 128] = piece[b : b + 1, :]

    factor = lax.rsqrt(ar_finish(2, ar_e) / WIDTH + EPS)
    f_row[...] = factor
    for b in range(3):
        fcol[pl.ds(b * 128, 128), :] = spread_rows(factor[b : b + 1, :])
    for r, (first, count) in enumerate(((0, 64), (64, 64), (128, 128), (256, 128))):
        part = h_e[pl.ds(first, count), :] * lanes4(fcol[pl.ds(first, count), :])
        vec[r : r + 1, :] = jnp.sum(part, axis=0, keepdims=True) * gain / count
    nt = (((1,), (1,)), ((), ()))
    vec_g[...] = vec[0:32, :] * gain
    sims = lax.dot_general(vec_g[...], h_e[...], nt, precision=HI, preferred_element_type=F32)
    gram = lax.dot_general(vec[0:8, :], vec[...], nt, precision=HI, preferred_element_type=F32)
    first = lax.broadcasted_iota(jnp.int32, (1, 128), 1) < 64
    ar_g[t, 0:8, :] = jnp.where(first, sims[8:16, 0:128], sims[16:24, 0:128])
    ar_g[t, 8:16, :] = jnp.zeros((8, 128), F32)
    ar_g[t, 8:9, :] = jnp.where(first, sims[0:1, 0:128], sims[1:2, 0:128])
    ar_g[t, 9:10, :] = jnp.where(first, sims[2:3, 0:128], sims[3:4, 0:128])
    ar_g[t, 10:11, :] = sims[0:1, 128:256]
    ar_g[t, 11:12, :] = sims[2:3, 128:256]
    ar_g[t, 12:13, :] = sims[1:2, 256:384]
    ar_g[t, 13:14, :] = sims[3:4, 256:384]
    ar_g[t, 16:24, :] = gram
    left = list(sent)
    sent.clear()
    ar_start(3, ar_g)
    for copy in left:
        copy.wait_send()
    both = ar_finish(3, ar_g)

    gram = both[16:24, :]
    row = lax.broadcasted_iota(jnp.int32, (8, 128), 0)
    lane = lax.broadcasted_iota(jnp.int32, (8, 128), 1)
    diag = jnp.where((lane == row) & (row < 4), gram, 0.0)
    norm_row = lax.rsqrt(jnp.sum(diag, axis=1, keepdims=True) / WIDTH + EPS)
    norm_lane = lax.rsqrt(jnp.sum(diag, axis=0, keepdims=True) / WIDTH + EPS)
    norm_lane = jnp.where(lane < 4, norm_lane, 1.0)
    unit = gram * norm_row * norm_lane
    is_pos = (lane == row + 2) & (row < 2)
    is_neg = (lane >= 8 + 8 * row) & (lane < 16 + 8 * row) & (row < 2)
    pos = jnp.sum(jnp.where(is_pos, unit, 0.0), axis=1, keepdims=True) * SCALE
    exp_neg = jnp.where(is_neg, jnp.exp(jnp.where(is_neg, unit, 0.0) * SCALE), 0.0)
    exp_pos = jnp.exp(pos)
    total = exp_pos + jnp.sum(exp_neg, axis=1, keepdims=True)
    terms = jnp.where(row < 2, jnp.log(total) - pos, 0.0)
    loss = jnp.sum(terms, axis=0, keepdims=True)
    d_pos = jnp.where(is_pos, exp_pos / total - 1.0, 0.0)
    pos_lane = jnp.sum(d_pos, axis=0, keepdims=True)
    pos_row = jnp.sum(jnp.where(lane == row, pos_lane, 0.0), axis=1, keepdims=True)
    coef = d_pos + exp_neg / total
    coef = coef + jnp.where((lane == row - 2) & (row < 4), pos_row, 0.0)
    coef = coef * SCALE
    back = jnp.sum(coef * unit, axis=1, keepdims=True) / WIDTH
    coef = norm_row * (coef * norm_lane - jnp.where(lane == row, back * norm_row, 0.0))
    coef = jnp.where(row < 4, coef, 0.0)
    coef = coef / jnp.where(row < 2, 64.0, 128.0)

    l_c[core] = jnp.broadcast_to(loss, (8, 128))
    pair_loss = remote(
        l_c.at[core], l_c.at[core], ls_sems, (0,), grp_of(lo, x, 1 - core)
    )
    pair_loss.start()

    s_full[8:16, 0:128] = both[0:8, :]
    s_full[16:24, 0:128] = both[0:8, :]
    s_full[0:2, 0:128] = jnp.broadcast_to(both[8:9, :], (2, 128))
    s_full[2:4, 0:128] = jnp.broadcast_to(both[9:10, :], (2, 128))
    s_full[0:1, 128:256] = both[10:11, :]
    s_full[2:3, 128:256] = both[11:12, :]
    s_full[1:2, 256:384] = both[12:13, :]
    s_full[3:4, 256:384] = both[13:14, :]
    inner = jnp.dot(coef, s_full[...], precision=HI, preferred_element_type=F32)
    urow[...] = jnp.dot(coef, vec[...], precision=HI, preferred_element_type=F32) * gain
    wanted = (
        ((row == 0) & (lane < 64)) | ((row == 1) & (lane >= 64)),
        row == 2,
        row == 3,
    )
    for b in range(3):
        line = jnp.sum(
            jnp.where(wanted[b], inner[:, b * 128 : b * 128 + 128], 0.0), axis=0, keepdims=True
        )
        f = f_row[b : b + 1, :]
        gcol[pl.ds(b * 128, 128), :] = spread_rows(line * f * f / WIDTH)
    for r, (first, count) in enumerate(((0, 64), (64, 64), (128, 128), (256, 128))):
        at = pl.ds(first, count)
        part = urow[r : r + 1, :] - h_e[at, :] * lanes4(gcol[at, :])
        dh[at, :] = (lanes4(fcol[at, :]) * part).astype(BF16)

    def pc_copy(i, x_):
        return remote(
            psend.at[x_], precv.at[x_], pc_sems, (i,), grp_of(lo, x, 1 - core)
        )

    up = (1, -1, 1, -1)
    line_of = (3 * (1 - lo // 2), 2 - lo // 2, lo + 1 - 2 * (lo % 2), lo)

    def px_copy(stage, side, d):
        at = stage + side
        return remote(
            xsend.at[at, d], xrecv.at[at, d], px_sems, (at, d),
            grp_of(lo, (x + (up[d], 1, -1)[at] + 4) % 4, core),
        )

    def pz_copy(k):
        d = (line_of[k] - lo + 4) % 4
        return remote(
            zsend.at[k], zrecv.at[d], pz_sems, (d,), grp_of(line_of[k], x, core)
        )

    def pz_arrival(d):
        return remote(zsend.at[d], zrecv.at[d], pz_sems, (d,), grp_of(lo, x, core))

    turns = (2, 1, 3, 0)

    def part_of(x_, c_):
        rows = a_t[pl.ds((x_ * 2 + c_) * 4, 4)].reshape(512, ETOK)
        part = jnp.dot(rows, dh[...], preferred_element_type=F32)
        return part.reshape(4, 128, COLS)

    def give(i):
        x_ = (x + turns[i]) % 4
        psend[x_] = part_of(x_, 1 - core).astype(BF16)
        pc_copy(i, x_).start()

    def keep(i):
        x_ = (x + turns[i]) % 4
        own[x_] = part_of(x_, core)

    def pair_sum(x_, d):
        l_ = line_of[d]
        return own[x_, l_] + precv[x_, l_].astype(F32)

    def direct(d):
        side = 0 if up[d] == -1 else 1
        xsend[1 + side, d] = pair_sum((x + (1, 3)[side]) % 4, d).astype(BF16)
        px_copy(1, side, d).start()

    def relay(d):
        side = 0 if up[d] == 1 else 1
        px_copy(0, 0, d).wait_recv()
        total = pair_sum((x + (1, 3)[side]) % 4, d) + xrecv[0, d].astype(F32)
        xsend[1 + side, d] = total.astype(BF16)
        px_copy(1, side, d).start()

    give(0)
    keep(0)
    give(1)
    pair_loss.wait_recv()
    l_x[x] = l_c[0] + l_c[1]

    def lx_copy(d, slot):
        return remote(
            l_x.at[slot], l_x.at[slot], ls_sems, (d,), grp_of(lo, (x + d) % 4, core)
        )

    def lz_copy(d, slot):
        return remote(
            l_z.at[slot], l_z.at[slot], ls_sems, (3 + d,),
            grp_of((lo + d) % 4, x, core),
        )

    for d in (1, 2, 3):
        lx_copy(d, x).start()
    pc_copy(0, x).wait_recv()
    for d in range(4):
        xsend[0, d] = pair_sum((x + 2) % 4, d).astype(BF16)
        px_copy(0, 0, d).start()
    keep(1)
    give(2)
    keep(2)
    give(3)
    pc_copy(1, x).wait_recv()
    pc_copy(2, x).wait_recv()
    left = list(sent[:8])
    del sent[:8]
    for copy in left:
        copy.wait_send()
    relay(0)
    relay(1)
    direct(1)
    direct(0)
    keep(3)
    for d in (1, 2, 3):
        lx_copy(d, (x - d + 4) % 4).wait_recv()
    l_z[lo] = (l_x[0] + l_x[1]) + (l_x[2] + l_x[3])
    for d in (1, 2, 3):
        lz_copy(d, lo).start()
    relay(2)
    direct(2)
    direct(3)
    relay(3)
    pc_copy(3, x).wait_recv()
    for d in range(4):
        total = pair_sum(x, d)
        for side in (0, 1):
            px_copy(1, side, d).wait_recv()
        total = total + (xrecv[1, d].astype(F32) + xrecv[2, d].astype(F32))
        if d == 3:
            grad_ref[...] = total
        else:
            zsend[d] = total.astype(BF16)
            pz_copy(d).start()
    for d in (1, 2, 3):
        lz_copy(d, (lo - d + 4) % 4).wait_recv()
    loss_ref[...] = ((l_z[0] + l_z[1]) + (l_z[2] + l_z[3]))[0:1, 0:1] / 64.0
    for d in (1, 3, 2):
        pz_arrival(d).wait_recv()
    grad_ref[...] += (zrecv[1].astype(F32) + zrecv[2].astype(F32)) + zrecv[3].astype(F32)

    for copy in sent:
        copy.wait_send()


def shards(
    q_attn, q_resid, p_attn, p_resid, w_out, w_snap, norm_gain, pass_attn, pass_resid,
    pass_len, block_owner, neg_ids,
):
    hbm = pl.BlockSpec(memory_space=pl.ANY)
    vmem = pl.BlockSpec(memory_space=pltpu.VMEM)
    smem = pl.BlockSpec(memory_space=pltpu.SMEM)
    dma = pltpu.SemaphoreType.DMA

    def both(shape):
        return (dma(shape), dma(shape))

    loss, grad, index = pl.pallas_call(
        kernel,
        out_shape=(
            jax.ShapeDtypeStruct((1, 1), F32),
            jax.ShapeDtypeStruct((128, COLS), F32),
            jax.ShapeDtypeStruct((2, COLS), BF16),
        ),
        in_specs=[hbm] * 6 + [vmem] + [hbm] * 2 + [smem] * 3,
        out_specs=(vmem, vmem, vmem),
        scratch_shapes=[
            pltpu.VMEM((8, STOK, COLS), BF16),
            pltpu.VMEM((8, ETOK, COLS), BF16),
            pltpu.VMEM((32, 128, COLS), BF16),
            pltpu.VMEM((32, 128, COLS), BF16),
            pltpu.VMEM((STOK, COLS), BF16),
            pltpu.VMEM((ETOK, COLS), BF16),
            pltpu.VMEM((STOK, COLS), F32),
            pltpu.VMEM((ETOK, COLS), F32),
            pltpu.VMEM((32, 128, ETOK), BF16),
            pltpu.VMEM((8, 8, 128), F32),
            pltpu.VMEM((8, 8, 128), F32),
            pltpu.VMEM((8, 8, 128), F32),
            pltpu.VMEM((8, 24, 128), F32),
            pltpu.VMEM((4, 8, 8, 128), F32),
            pltpu.VMEM((8, COLS), F32),
            pltpu.VMEM((128, COLS), F32),
            pltpu.VMEM((32, COLS), F32),
            pltpu.VMEM((128, ETOK), F32),
            pltpu.VMEM((ETOK, 128), F32),
            pltpu.VMEM((ETOK, 128), F32),
            pltpu.VMEM((8, 128), F32),
            pltpu.VMEM((8, COLS), F32),
            pltpu.VMEM((ETOK, COLS), BF16),
            pltpu.VMEM((4, 4, 128, COLS), F32),
            pltpu.VMEM((4, 4, 128, COLS), BF16),
            pltpu.VMEM((4, 4, 128, COLS), BF16),
            pltpu.VMEM((3, 4, 128, COLS), BF16),
            pltpu.VMEM((3, 4, 128, COLS), BF16),
            pltpu.VMEM((4, 128, COLS), BF16),
            pltpu.VMEM((4, 128, COLS), BF16),
            pltpu.VMEM((2, 8, 128), F32),
            pltpu.VMEM((4, 8, 128), F32),
            pltpu.VMEM((4, 8, 128), F32),
            dma((8,)),
            both((2, PARTS, 3)),
            both((PARTS,)),
            both((2, 2, 3)),
            both((2, 7, 4)),
            both((2, 7, 4)),
            both((4, 8)),
            both((7,)),
            both((4,)),
            both((3, 4)),
            both((4,)),
            both((7,)),
        ],
        compiler_params=pltpu.CompilerParams(
            collective_id=0, has_side_effects=True, vmem_limit_bytes=56 * 2**20
        ),
    )(
        q_attn.reshape(128, COLS),
        q_resid.reshape(128, COLS),
        p_attn.reshape(256, COLS),
        p_resid.reshape(256, COLS),
        w_out,
        w_snap,
        norm_gain,
        pass_attn.reshape(STOK, COLS),
        pass_resid.reshape(STOK, COLS),
        pass_len,
        block_owner,
        neg_ids,
    )
    return (loss[0, 0], grad, index)


def solution(mesh):
    placed = (
        P("grp", None, "tp"),
        P("grp", None, "tp"),
        P("grp", None, "tp"),
        P("grp", None, "tp"),
        P("grp", "tp"),
        P("grp", "tp"),
        P("tp"),
        P("grp", None, "tp"),
        P("grp", None, "tp"),
        P("grp"),
        P(),
        P("grp", None),
    )
    return jax.shard_map(
        shards,
        mesh=mesh,
        in_specs=placed,
        out_specs=(P(), P("grp", "tp"), P("grp", "tp")),
        check_vma=False,
    )
```
